32 devices in a mesh: grp: 4 (over x, core), tile: 8 (over z, y).
Axes of the slice: x: 2, y: 2, z: 4, core: 2. Of those that a mesh axis runs over, the one named last changes fastest.
Arguments:
- start_velocity: float32 [2, 128, 4096], P(None, 'grp', 'tile'), may hold values from -6 to 6
- driving_stress: float32 [2, 128, 4096], P(None, 'grp', 'tile'), may hold values from -6 to 6
- viscosity: float32 [2, 128, 4096], P(None, 'grp', 'tile'), may hold values from 0.3 to 3
- friction: float32 [128, 4096], P('grp', 'tile'), may hold values from 0.02 to 0.5
- cell_element: int32 [128, 4096], P('grp', 'tile'), may hold values from 0 to 4095, as said below
- observed: float32 [16384, 256], P(('grp', 'tile')), may hold values from -6 to 6
- look: float32 [2, 16384, 256], P(None, ('grp', 'tile')), may hold values from -3 to 3
- row_owner: int32 [16384, 1], P(('grp', 'tile')), may hold values from 0 to 31; in each aligned block of 512 rows (0 to 511, 512 to 1023, ...) at most 32 rows name the same one
- row_cell: int32 [16384], P(('grp', 'tile')), may hold values from 0 to 16383
Outputs:
- stress_adjoint: float32 [2, 128, 4096], P(None, 'grp', 'tile')
- friction_adjoint: float32 [4096], P(('grp', 'tile'))
The draws below stay inside these ranges and needn't reach their ends.
Inputs may be any that keep to these rules, and one draw needn't show every extreme that they name: `row_owner`: of the 512 rows of one device at most 32 name the same owner, and in some blocks one owner is named by exactly 32 rows. `cell_element`: the element of a node held by the device with grp index g lies in g * 128 * 8 to (g + 1) * 128 * 8 - 1; element e is owned by the device at flattened index e // 128.
All inputs are finite; a program needn't handle non-finite values.
Results may differ from the reference program's by a relative error of at most 0.00002.
Values sent between devices are 32-bit elements; how exact they have to be, the bound alone decides.
No kernel may reach another device: no remote copies, remote signals or barrier semaphores. Data moves between devices by JAX's collectives and lax.ppermute only.
A program may use at most 128 MiB of HBM per device.

```python
import math
import jax
import jax.numpy as jnp
import numpy as np

CX = 32
CY = 512
R_DEV = 512
EPOCHS = 256
SWEEPS = 8
PICARD = 2
NX = 128
NY = 4096
ROWS = 16384
CAP = 32
ELEMENTS = 4096
N_TILE = 8
DEVICES = 32


def draw_cell_element(key, part):
    group_width = CX * NY // 128
    rows_i = jnp.arange(NX, dtype=jnp.int32)[:, None]
    within = jax.random.randint(key, (NX, NY), 0, group_width)
    return (rows_i // CX * group_width + within).astype(jnp.int32)


def with_ends(values, rng, low, largest):
    longest = values.shape.index(max(values.shape))
    spots = []
    for shift in (0, 1):
        where = [jax.random.randint(jax.random.fold_in(rng, axis), (), 0, length) for axis, length in enumerate(values.shape)]
        where[longest] = (where[longest] + shift) % values.shape[longest]
        spots.append(tuple(where))
    return values.at[spots[0]].set(low).at[spots[1]].set(largest)


def steps_of(key, extent, cuts, low, high):
    factor_of = 1.0
    for position, shards_of in cuts:
        draws = jax.random.uniform(jax.random.fold_in(jax.random.fold_in(key, 6), position), (shards_of,), jnp.float32, low / len(cuts), high / len(cuts))
        factor_of = factor_of * jnp.repeat(jnp.exp(draws), extent[position] // shards_of).reshape((-1,) + (1,) * (len(extent) - 1 - position))
    return factor_of


def assign_block(stream_key, own, number, rows, number_of, top, reach, skew):
    order = jax.random.permutation(stream_key, number_of)
    crowded, ordinary = portions_of(number_of, rows * top, reach, skew, True), portions_of(number_of, rows * top, reach, skew, False)
    places = jnp.arange(number_of)

    def named(tallies, rotation):
        used = int((tallies > 0).sum())
        fixed = max(1, used // 4)
        moved = fixed + (places - fixed + rotation * (used - fixed)) % max(1, number_of - fixed)
        return jnp.zeros((number_of,), jnp.int32).at[order[jnp.where(places < fixed, places, moved)]].set(jnp.asarray(tallies, jnp.int32))

    tallies = jnp.where(number % 4 == 0, named(crowded, number // 4), named(ordinary, number - number // 4 - 1))
    mixed = jax.random.permutation(jax.random.fold_in(own, 3), number_of)
    giver, taker = mixed[0:number_of // 2 * 2:2], mixed[1:number_of // 2 * 2:2]
    margin = jnp.minimum(tallies[giver] - 1, reach - tallies[taker]) // 2
    margin = jnp.where((giver == order[0]) | (taker == order[0]) | (tallies[taker] == 0), 0, jnp.maximum(margin, 0))
    moved = jax.random.randint(jax.random.fold_in(own, 4), (number_of // 2,), 0, 1 << 20) % (margin + 1)
    tallies = tallies.at[giver].add(-moved).at[taker].add(moved)
    members = jnp.searchsorted(jnp.cumsum(tallies), jnp.arange(rows * top), side="right").astype(jnp.int32)
    grid = members.reshape(top, rows).T
    grid = grid[jax.random.permutation(jax.random.fold_in(own, 1), rows)]
    rotation = jax.random.randint(jax.random.fold_in(own, 2), (rows, 1), 0, top)
    return jnp.take_along_axis(grid, (jnp.arange(top)[None, :] + rotation) % top, axis=1)


def portions_of(amount, total, limit, skew, full):
    weights = [(1 << 20) // math.isqrt(rank ** skew) + 1 for rank in range(1, amount + 1)]
    largest = limit if full else min(limit, max(-(-total // amount), total * weights[0] // sum(weights)))
    least = 1 if total - largest >= amount - 1 else 0
    given, surplus = [largest] + [least] * (amount - 1), total - largest - least * (amount - 1)
    while surplus > 0:
        candidates = [i for i in range(1, amount) if given[i] < largest] or [i for i in range(1, amount) if given[i] < limit]
        whole, left = sum([weights[i] for i in candidates]), surplus
        for i in candidates:
            addition = min(limit - given[i], max(1, left * weights[i] // whole), surplus)
            given[i] = given[i] + addition
            surplus = surplus - addition
    return np.array(given)


def gaussian(stream_key, dims, width, bound, shards=(), held_as=jnp.bfloat16):
    values = width * jax.random.normal(stream_key, dims, jnp.float32)
    if shards:
        values = values * steps_of(stream_key, dims, shards, -0.22, 0.18)
    return jnp.clip(values, -bound, bound).astype(held_as)


def setup_inputs(seed: int = 0) -> dict:
    key_of = jax.random.split(jax.random.key(seed), 10)
    start_velocity = gaussian(key_of[0], (2, NX, NY), 1.0, 6.0, ((1, 4), (2, 8)), jnp.float32)
    driving_stress = gaussian(key_of[1], (2, NX, NY), 1.0, 6.0, ((1, 4), (2, 8)), jnp.float32)
    viscosity = jnp.clip(jnp.exp(math.log(3.0) - 2.3025851 * jax.random.uniform(key_of[2], (PICARD, NX, NY), jnp.float32) ** steps_of(key_of[2], (PICARD, NX, NY), ((1, 4), (2, 8)), -0.2, 0.2)), 0.3, 3.0)
    friction = jnp.clip(jnp.exp(math.log(0.5) - 3.218876 * jax.random.uniform(key_of[3], (NX, NY), jnp.float32) ** steps_of(key_of[3], (NX, NY), ((0, 4), (1, 8)), -0.2, 0.2)), 0.02, 0.5)
    cell_element = draw_cell_element(jax.random.fold_in(key_of[9], 71), 0)
    observed = gaussian(key_of[5], (ROWS, EPOCHS), 1.0, 6.0, ((0, 32),), jnp.float32)
    look = gaussian(key_of[6], (2, ROWS, EPOCHS), 0.5, 3.0, ((1, 32),), jnp.float32)
    row_owner_keys = jax.random.split(jax.random.fold_in(key_of[7], 1), ROWS // R_DEV)
    row_owner_turns = jax.random.permutation(jax.random.fold_in(key_of[7], 3), ROWS // R_DEV)
    row_owner = jax.vmap(lambda own, number: assign_block(jax.random.fold_in(key_of[7], 2), own, number, R_DEV, DEVICES, 1, CAP, 2))(row_owner_keys, row_owner_turns).reshape((ROWS, 1))
    row_cell = with_ends(jax.random.randint(key_of[8], (ROWS,), 0, CX * CY), jax.random.fold_in(key_of[8], 1), 0, (CX * CY) - 1).astype(jnp.int32)
    return {"start_velocity": start_velocity, "driving_stress": driving_stress, "viscosity": viscosity, "friction": friction, "cell_element": cell_element, "observed": observed, "look": look, "row_owner": row_owner, "row_cell": row_cell}


def grad_x(p):
    return 0.5 * (p[1:, 1:] + p[1:, :-1] - p[:-1, 1:] - p[:-1, :-1])

def grad_y(p):
    return 0.5 * (p[1:, 1:] + p[:-1, 1:] - p[1:, :-1] - p[:-1, :-1])

def spread_x(t):
    return 0.5 * (t[:-1, :-1] + t[:-1, 1:] - t[1:, :-1] - t[1:, 1:])

def spread_y(t):
    return 0.5 * (t[:-1, :-1] + t[1:, :-1] - t[:-1, 1:] - t[1:, 1:])

def corner_mean(e):
    return 0.25 * (e[1:, 1:] + e[1:, :-1] + e[:-1, 1:] + e[:-1, :-1])

def operate(padded, quad_visc, friction_eff):
    values = padded[:, 1:-1, 1:-1]
    u_dx = grad_x(padded[0])
    u_dy = grad_y(padded[0])
    v_dx = grad_x(padded[1])
    v_dy = grad_y(padded[1])
    stress_xx = quad_visc * (4.0 * u_dx + 2.0 * v_dy)
    stress_yy = quad_visc * (4.0 * v_dy + 2.0 * u_dx)
    stress_xy = quad_visc * (u_dy + v_dx)
    first = spread_x(stress_xx) + spread_y(stress_xy) + friction_eff * values[0]
    second = spread_y(stress_yy) + spread_x(stress_xy) + friction_eff * values[1]
    return jnp.stack([first, second])

def one_sweep(velocity, quad_visc, friction_eff, precond, stress):
    padded = jnp.pad(velocity, ((0, 0), (1, 1), (1, 1)))
    return velocity + precond * (stress - operate(padded, quad_visc, friction_eff))

def reference(start_velocity, driving_stress, viscosity, friction, cell_element, observed, look, row_owner, row_cell):
    padded_visc = jnp.pad(viscosity, ((0, 0), (1, 1), (1, 1)))
    quad_list = [corner_mean(padded_visc[picard]) for picard in range(PICARD)]
    owner_dev = row_owner[:, 0].astype(jnp.int32)
    cell_index = (owner_dev // N_TILE * CX + row_cell // CY) * NY + owner_dev % N_TILE * CY + row_cell % CY
    sweep_fn = jax.checkpoint(one_sweep)

    def misfit(stress, log_factor):
        friction_eff = friction * jnp.exp(log_factor[cell_element])
        velocity = start_velocity
        for picard in range(PICARD):
            quad_visc = quad_list[picard]
            diagonal = 1.25 * (quad_visc[:-1, :-1] + quad_visc[:-1, 1:] + quad_visc[1:, :-1] + quad_visc[1:, 1:]) + friction_eff
            precond = 0.45 / diagonal
            for _ in range(SWEEPS):
                velocity = sweep_fn(velocity, quad_visc, friction_eff, precond, stress)
        speeds = velocity.reshape(2, NX * NY)[:, cell_index]
        misfit_rows = look[0] * speeds[0][:, None] + look[1] * speeds[1][:, None] - observed
        return 0.5 * jnp.sum(misfit_rows * misfit_rows) / math.sqrt(EPOCHS)
    value, pullback = jax.vjp(misfit, driving_stress, jnp.zeros((ELEMENTS,), jnp.float32))
    stress_adjoint, friction_adjoint = pullback(jnp.ones_like(value))
    return (stress_adjoint, friction_adjoint)
```

```python
import math

import jax
import jax.numpy as jnp
from jax import lax
from jax.experimental import pallas as pl
from jax.experimental.pallas import tpu as pltpu
from jax.sharding import PartitionSpec as P

SWEEPS = 8
PICARD = 2
LANES = 128
FIELDS = 7
REACH = 32
CHUNK = 64
CHUNKS = 8
STRIP = 16
VMEM_BYTES = 60 * 1024 * 1024
NT = (((1,), (1,)), ((), ()))


def halo_pair(block, axis):
    count = lax.axis_size(axis)
    forward = [(i, i + 1) for i in range(count - 1)]
    backward = [(target, source) for source, target in forward]
    return lax.ppermute(block, axis, forward), lax.ppermute(block, axis, backward)


def thirds(values):
    first = values.astype(jnp.bfloat16)
    rest = values - first.astype(jnp.float32)
    second = rest.astype(jnp.bfloat16)
    third = (rest - second.astype(jnp.float32)).astype(jnp.bfloat16)
    return first, second, third


def one_hot(mask):
    return jnp.where(mask, 1.0, 0.0).astype(jnp.bfloat16)


def rows_kernel(groups, tiles, cap, look_ref, obs_ref, owner_ref, cell_ref, out_ref, pad_ref):
    rows = obs_ref.shape[0]
    devices = groups * tiles
    look_x, look_y, obs = look_ref[0], look_ref[1], obs_ref[...]
    lane = lax.broadcasted_iota(jnp.int32, (rows, LANES), 1)
    sums = jnp.zeros((rows, LANES), jnp.float32)
    for place, (a, b) in enumerate(
        ((look_x, look_x), (look_x, look_y), (look_y, look_y), (look_x, obs), (look_y, obs))
    ):
        sums = jnp.where(lane == place, jnp.sum(a * b, axis=1, keepdims=True), sums)
    sums = sums.T[:8]
    owner = owner_ref[...]
    cell = cell_ref[...]
    named = lax.broadcasted_iota(jnp.int32, (devices, rows), 0) == owner
    before = lax.broadcasted_iota(jnp.int32, (rows, rows), 0) < lax.broadcasted_iota(
        jnp.int32, (rows, rows), 1
    )
    ranks = jnp.dot(one_hot(named), one_hot(before), preferred_element_type=jnp.float32)
    rank = jnp.sum(jnp.where(named, ranks, 0.0), axis=0, keepdims=True)
    slot = owner * cap + rank.astype(jnp.int32)
    hit = one_hot(lax.broadcasted_iota(jnp.int32, (devices * cap, rows), 0) == slot)
    cells = jnp.concatenate(
        [
            lax.shift_right_logical(cell, 7),
            jnp.bitwise_and(cell, 127),
            jnp.zeros((6, rows), jnp.int32),
        ],
        axis=0,
    ).astype(jnp.float32)
    s0, s1, s2 = thirds(sums)
    left = jnp.concatenate(
        [s0.astype(jnp.float32), s1.astype(jnp.float32), s2.astype(jnp.float32), cells], axis=0
    ).astype(jnp.bfloat16)
    placed = lax.dot_general(left, hit, NT, preferred_element_type=jnp.float32)
    table = placed[:8] + placed[8:16] + placed[16:24]
    row = lax.broadcasted_iota(jnp.int32, table.shape, 0)
    table = jnp.where(row == 5, placed[24:25] * 128.0 + placed[25:26], table)
    edge = jnp.zeros((8, LANES), jnp.float32)
    pad_ref[:, :LANES] = edge
    pad_ref[:, LANES : LANES + devices * cap] = table
    pad_ref[:, LANES + devices * cap :] = edge
    lane8 = lax.broadcasted_iota(jnp.int32, (8, LANES), 1)
    for g in range(groups):
        for t in range(tiles):
            start = (g * tiles + t - 1) * cap + LANES
            base, off = start // LANES * LANES, start % LANES
            piece = pad_ref[:, base : base + LANES]
            if off:
                after = pad_ref[:, base + LANES : base + 2 * LANES]
                piece = jnp.where(
                    lane8 < LANES - off,
                    pltpu.roll(piece, LANES - off, 1),
                    pltpu.roll(after, LANES - off, 1),
                )
            low = cap if t == 0 else 0
            high = 2 * cap if t == tiles - 1 else 3 * cap
            piece = jnp.where((lane8 >= low) & (lane8 < high), piece, 0.0)
            for d in range(3):
                goal = g - (d - 1)
                if 0 <= goal < groups:
                    out_ref[goal * tiles + t, d * 8 : d * 8 + 8, :] = piece
    for t in range(tiles):
        out_ref[t, 0:8, :] = edge
        out_ref[(groups - 1) * tiles + t, 16:24, :] = edge


def pack_rows(groups, tiles, look, observed, row_owner, row_cell):
    rows = observed.shape[0]
    devices = groups * tiles
    cap = max(2, 2 * rows // devices)
    return pl.pallas_call(
        lambda *refs: rows_kernel(groups, tiles, cap, *refs),
        out_shape=jax.ShapeDtypeStruct((devices, 24, LANES), jnp.float32),
        scratch_shapes=[pltpu.VMEM((8, devices * cap + 2 * LANES), jnp.float32)],
        compiler_params=pltpu.CompilerParams(vmem_limit_bytes=VMEM_BYTES),
        cost_estimate=pl.CostEstimate(flops=4_000_000, bytes_accessed=4_000_000, transcendentals=0),
        name="row_sums",
    )(look, observed, row_owner.reshape(1, rows), row_cell.reshape(1, rows))


def nodes_kernel(cap, rows_x, rows_y, in_ref, mid_ref, side_ref, left_ref, right_ref):
    devices = in_ref.shape[0]
    per = LANES // cap
    slots = devices * cap
    shift = rows_y.bit_length() - 1
    lane8 = lax.broadcasted_iota(jnp.int32, (8, LANES), 1)
    for d in range(3):
        wide = rows_x if d == 1 else STRIP
        first_x = {0: rows_x - STRIP, 1: 0, 2: 0}[d]
        out_x = {0: 0, 1: STRIP, 2: STRIP + rows_x}[d]
        lists = []
        for dt in range(3):
            parts = []
            for j in range(devices // per):
                part = jnp.zeros((8, LANES), jnp.float32)
                for q in range(per):
                    source = in_ref[j * per + q, d * 8 : d * 8 + 8, :]
                    turn = (q - dt) * cap % LANES
                    moved = pltpu.roll(source, turn, 1) if turn else source
                    part = jnp.where((lane8 >= q * cap) & (lane8 < q * cap + cap), moved, part)
                parts.append(part)
            lists.append(jnp.concatenate(parts, axis=1))
        for where, out_ref, width in (((1,), mid_ref, rows_y), ((0, 2), side_ref, LANES)):
            for position, dt in enumerate(where):
                values = lists[dt]
                cell = values[5:6].astype(jnp.int32)
                cell_x = lax.shift_right_logical(cell, shift) - first_x
                cell_y = jnp.bitwise_and(cell, rows_y - 1)
                begin = position * slots
                in_x = lax.broadcasted_iota(jnp.int32, (wide, slots), 0) == cell_x
                pieces = thirds(values)
                for p in range(3):
                    piece = pieces[p].astype(jnp.float32)
                    for f in range(5):
                        at = (p * 5 + f) * wide
                        left_ref[at : at + wide, begin : begin + slots] = jnp.where(
                            in_x, piece[f : f + 1], 0.0
                        ).astype(jnp.bfloat16)
                if dt == 0:
                    cell_y = cell_y - (rows_y - LANES)
                    cell_y = jnp.where(cell_y >= LANES - STRIP, cell_y, -1)
                if dt == 2:
                    cell_y = jnp.where(cell_y < STRIP, cell_y, -1)
                right_ref[:width, begin : begin + slots] = one_hot(
                    lax.broadcasted_iota(jnp.int32, (width, slots), 0) == cell_y
                )
            total = len(where) * slots
            added = lax.dot_general(
                left_ref[: 15 * wide, :total],
                right_ref[:width, :total],
                NT,
                preferred_element_type=jnp.float32,
            )
            added = added[: 5 * wide] + added[5 * wide : 10 * wide] + added[10 * wide :]
            for f in range(5):
                out_ref[f, out_x : out_x + wide, :] = added[f * wide : (f + 1) * wide]


def add_on_nodes(arrived, cap, rows_x, rows_y):
    slots = arrived.shape[0] * cap
    high = rows_x + 2 * STRIP
    return pl.pallas_call(
        lambda *refs: nodes_kernel(cap, rows_x, rows_y, *refs),
        out_shape=(
            jax.ShapeDtypeStruct((5, high, rows_y), jnp.float32),
            jax.ShapeDtypeStruct((5, high, LANES), jnp.float32),
        ),
        scratch_shapes=[
            pltpu.VMEM((15 * rows_x, 2 * slots), jnp.bfloat16),
            pltpu.VMEM((rows_y, 2 * slots), jnp.bfloat16),
        ],
        compiler_params=pltpu.CompilerParams(vmem_limit_bytes=VMEM_BYTES),
        cost_estimate=pl.CostEstimate(flops=4_000_000, bytes_accessed=4_000_000, transcendentals=0),
        name="add_on_nodes",
    )(arrived)


def edges_kernel(low_ref, own_ref, high_ref, to_low_ref, to_high_ref):
    lane = lax.broadcasted_iota(jnp.int32, (8, LANES), 1)
    last = own_ref.shape[2] - LANES
    sources = (low_ref, own_ref, high_ref)
    for f in range(FIELDS):
        for b in range(3):
            begin = jnp.zeros((8, LANES), jnp.float32)
            end = jnp.zeros((8, LANES), jnp.float32)
            for k in range(4):
                block = 3 * k + b
                ref, at = sources[block // 4], block % 4 * 8
                mine = (lane >= 32 * k) & (lane < 32 * k + 32)
                head = ref[f, at : at + 8, :LANES]
                tail = ref[f, at : at + 8, last:]
                if k:
                    head = pltpu.roll(head, 32 * k, 1)
                if k != 3:
                    tail = pltpu.roll(tail, 32 * k + 32, 1)
                begin = jnp.where(mine, head, begin)
                end = jnp.where(mine, tail, end)
            to_low_ref[f, b * 8 : b * 8 + 8, :] = begin
            to_high_ref[f, b * 8 : b * 8 + 8, :] = end


def edges(low, own, high):
    shape = jax.ShapeDtypeStruct((FIELDS, 24, LANES), jnp.float32)
    return pl.pallas_call(
        edges_kernel,
        out_shape=(shape, shape),
        compiler_params=pltpu.CompilerParams(vmem_limit_bytes=VMEM_BYTES),
        cost_estimate=pl.CostEstimate(flops=500_000, bytes_accessed=500_000, transcendentals=0),
        name="edges",
    )(low, own, high)


def tile_rows(row, count=1):
    return slice(8 * row, 8 * (row + count))


def to_rows(pieces, left, right, store):
    lane = lax.broadcasted_iota(jnp.int32, (8, LANES), 1)
    by_32 = [left] + [pltpu.roll(p, 32, 1) for p in pieces]
    by_96 = [pltpu.roll(p, 96, 1) for p in pieces] + [right]
    for k in range(4):
        store(2 * k, jnp.where(lane < 32, by_32[k], by_32[k + 1]))
        store(2 * k + 1, jnp.where(lane < 96, by_96[k], by_96[k + 1]))


def from_rows(load):
    lane = lax.broadcasted_iota(jnp.int32, (8, LANES), 1)
    return [
        jnp.where(lane < CHUNK, pltpu.roll(load(2 * k), 96, 1), pltpu.roll(load(2 * k + 1), 32, 1))
        for k in range(4)
    ]


def stencil_rows(load_u, load_v, visc, first_row, last_row, finish):
    def lateral(row):
        u, v = load_u(row), load_v(row)
        u_next, v_next = pltpu.roll(u, LANES - 1, 1), pltpu.roll(v, LANES - 1, 1)
        return u, v, u + u_next, u_next - u, v + v_next, v_next - v

    def stresses(row, here, after):
        half, quarter = visc(row)
        x_u, y_u = after[2] - here[2], after[3] + here[3]
        x_v, y_v = after[4] - here[4], after[5] + here[5]
        both = x_u + y_v
        return half * (x_u + both), half * (y_v + both), quarter * (y_u + x_v)

    here = lateral(first_row)
    below = stresses(first_row - 1, lateral(first_row - 1), here)
    for row in range(first_row, last_row + 1):
        after = lateral(row + 1)
        above = stresses(row, here, after)
        a, c = below[0] - above[0], below[1] + above[1]
        b, e = below[2] + above[2], below[2] - above[2]
        first = pltpu.roll(a + b, 1, 1) + (a - b)
        second = pltpu.roll(c + e, 1, 1) + (e - c)
        finish(row, here[0], here[1], first, second)
        here, below = after, above


def solve_kernel(
    epochs,
    grp_count,
    tile_count,
    place_ref,
    own_ref,
    low_ref,
    high_ref,
    left_ref,
    right_ref,
    mid_ref,
    side_ref,
    ids_ref,
    out_ref,
    elem_ref,
    field,
    misfit,
    half_q,
    quarter_q,
    keep,
    prec,
    push,
    turn,
    wave_a,
    wave_b,
    seen,
    total,
    fric,
    terms,
):
    rows_x = own_ref.shape[1]
    height = rows_x + 2 * REACH
    grp, tile = place_ref[0], place_ref[1]

    sources = (low_ref, own_ref, high_ref)
    for f in range(FIELDS):
        for block in range(height // 8):
            ref, at = sources[block // 4], block % 4 * 8
            k, b = block // 3, block % 3
            left = left_ref[f, b * 8 : b * 8 + 8, :]
            right = right_ref[f, b * 8 : b * 8 + 8, :]
            if k:
                left = pltpu.roll(left, LANES - 32 * k, 1)
            if k != 3:
                right = pltpu.roll(right, 96 - 32 * k, 1)

            def store(s, value, f=f, block=block):
                field[f, pl.ds(64 * block + s, 8, stride=8), :] = value

            to_rows([ref[f, at : at + 8, LANES * j : LANES * j + LANES] for j in range(4)], left, right, store)
    for f in range(5):
        for block in range((rows_x + 2 * STRIP) // 8):
            at = block * 8
            beyond = side_ref[f, at : at + 8, :]

            def store(s, value, f=f, block=block):
                misfit[f, pl.ds(64 * block + s, 8, stride=8), :] = value

            to_rows(
                [mid_ref[f, at : at + 8, LANES * j : LANES * j + LANES] for j in range(4)],
                pltpu.roll(beyond, 32, 1),
                pltpu.roll(beyond, 96, 1),
                store,
            )

    lane = lax.broadcasted_iota(jnp.int32, (8, LANES), 1)
    chunk = lax.broadcasted_iota(jnp.int32, (8, LANES), 0)
    y = tile * (CHUNK * CHUNKS) + chunk * CHUNK + lane - 32
    in_y = (y >= 0) & (y < tile_count * (CHUNK * CHUNKS))
    in_low = in_y & jnp.broadcast_to(grp > 0, in_y.shape)
    in_high = in_y & jnp.broadcast_to(grp < grp_count - 1, in_y.shape)
    for p, (first_row, last_row) in enumerate(((2, height - 3), (2 + SWEEPS, height - 3 - SWEEPS))):

        def summed(row, p=p):
            e = field[4 + p, tile_rows(row), :]
            return e + pltpu.roll(e, LANES - 1, 1)

        before = summed(first_row - 1)
        row_sum = summed(first_row)
        quad = before + row_sum
        half_q[p, tile_rows(first_row - 1), :] = 0.125 * quad
        quarter_q[p, tile_rows(first_row - 1), :] = 0.0625 * quad
        quad_below = quad + pltpu.roll(quad, 1, 1)
        for row in range(first_row, last_row + 1):
            next_sum = summed(row + 1)
            quad = row_sum + next_sum
            half_q[p, tile_rows(row), :] = 0.125 * quad
            quarter_q[p, tile_rows(row), :] = 0.0625 * quad
            quad_above = quad + pltpu.roll(quad, 1, 1)
            fr = field[6, tile_rows(row), :]
            diagonal = (1.25 * 0.25) * (quad_below + quad_above) + fr
            inside = in_low if row < REACH else in_high if row >= REACH + rows_x else in_y
            pre = jnp.where(inside, 0.45 / diagonal, 0.0)
            prec[p, tile_rows(row), :] = pre
            keep[p, tile_rows(row), :] = 1.0 - pre * fr
            push[p, 0, tile_rows(row), :] = pre * field[2, tile_rows(row), :]
            push[p, 1, tile_rows(row), :] = pre * field[3, tile_rows(row), :]
            if p == 0:
                turn[tile_rows(row), :] = pre * (1.0 / 0.45)
            else:
                turn[tile_rows(row), :] = turn[tile_rows(row), :] * diagonal
            row_sum, quad_below = next_sum, quad_above

    def visc(p):
        return lambda row: (half_q[p, tile_rows(row), :], quarter_q[p, tile_rows(row), :])

    def forward(p, step, source, target, first_row, last_row):
        def finish(row, u, v, first, second):
            at = tile_rows(row)
            pre, rest = prec[p, at, :], keep[p, at, :]
            new_u = rest * u + push[p, 0, at, :] - pre * first
            new_v = rest * v + push[p, 1, at, :] - pre * second
            target(0, row, new_u)
            target(1, row, new_v)
            if REACH <= row < REACH + rows_x:
                here = pl.ds(8 * (row - REACH), 8)
                seen[step, 0, here, :] = u + (new_u - u) * (1.0 / 0.45)
                seen[step, 1, here, :] = v + (new_v - v) * (1.0 / 0.45)

        stencil_rows(lambda r: source(0, r), lambda r: source(1, r), visc(p), first_row, last_row, finish)

    def reader(ref):
        return lambda c, row: ref[c, tile_rows(row), :]

    def writer(ref):
        def write(c, row, value):
            ref[c, tile_rows(row), :] = value

        return write

    for c in range(2):
        wave_a[c] = field[c]
    for p in range(PICARD):
        rows = (2 + SWEEPS * p, height - 3 - SWEEPS * p)

        def pair(i, _, p=p, rows=rows):
            forward(p, SWEEPS * p + 2 * i, reader(wave_a), writer(wave_b), *rows)
            forward(p, SWEEPS * p + 2 * i + 1, reader(wave_b), writer(wave_a), *rows)
            return 0

        lax.fori_loop(0, SWEEPS // 2, pair, 0)

    first_row, last_row = 17, height - 18
    for row in range(first_row, last_row + 1):
        at, mis = tile_rows(row), tile_rows(row - (REACH - STRIP))
        u, v = wave_a[0, at, :], wave_a[1, at, :]
        cross = misfit[1, mis, :]
        scale = prec[1, at, :] * (1.0 / math.sqrt(epochs))
        wave_a[0, at, :] = scale * (misfit[0, mis, :] * u + cross * v - misfit[3, mis, :])
        wave_a[1, at, :] = scale * (cross * u + misfit[2, mis, :] * v - misfit[4, mis, :])
    total[...] = jnp.zeros_like(total)
    fric[...] = jnp.zeros_like(fric)

    def gather(step, source):
        for row in range(REACH, REACH + rows_x):
            here = tile_rows(row - REACH)
            u, v = source(0, row), source(1, row)
            total[0, here, :] = total[0, here, :] + u
            total[1, here, :] = total[1, here, :] + v
            fric[here, :] = fric[here, :] - (u * seen[step, 0, here, :] + v * seen[step, 1, here, :])

    def backward(p, step, source, target, first_row, last_row, switch=False):
        def finish(row, u, v, first, second):
            at = tile_rows(row)
            pre, rest = prec[p, at, :], keep[p, at, :]
            new_u, new_v = rest * u - pre * first, rest * v - pre * second
            if switch:
                new_u, new_v = new_u * turn[at, :], new_v * turn[at, :]
            target(0, row, new_u)
            target(1, row, new_v)
            if REACH <= row < REACH + rows_x:
                here = tile_rows(row - REACH)
                total[0, here, :] = total[0, here, :] + u
                total[1, here, :] = total[1, here, :] + v
                fric[here, :] = fric[here, :] - (u * seen[step, 0, here, :] + v * seen[step, 1, here, :])

        stencil_rows(lambda r: source(0, r), lambda r: source(1, r), visc(p), first_row, last_row, finish)

    for p in range(PICARD - 1, -1, -1):
        edge = 18 if p == PICARD - 1 else 18 + SWEEPS
        rows = (edge, height - 1 - edge)
        top = SWEEPS * (p + 1) - 1

        def pair(i, _, p=p, rows=rows, top=top):
            backward(p, top - 2 * i, reader(wave_a), writer(wave_b), *rows)
            backward(p, top - 2 * i - 1, reader(wave_b), writer(wave_a), *rows)
            return 0

        lax.fori_loop(0, SWEEPS // 2 - 1, pair, 0)
        backward(p, top - SWEEPS + 2, reader(wave_a), writer(wave_b), *rows)
        if p:
            backward(p, top - SWEEPS + 1, reader(wave_b), writer(wave_a), *rows, switch=True)
        else:
            gather(0, reader(wave_b))

    for block in range(rows_x // 8):
        at = slice(block * 8, block * 8 + 8)
        for c in range(2):
            tiles = from_rows(lambda s: total[c, pl.ds(64 * block + s, 8, stride=8), :])
            for k in range(4):
                out_ref[c, at, LANES * k : LANES * k + LANES] = tiles[k]
        tiles = from_rows(lambda s: fric[pl.ds(64 * block + s, 8, stride=8), :])
        for k in range(4):
            terms[at, LANES * k : LANES * k + LANES] = (
                tiles[k] * own_ref[6, at, LANES * k : LANES * k + LANES]
            )

    owners, elems = elem_ref.shape
    first_element = grp * (owners * elems)
    width = ids_ref.shape[1]
    owner_at = lax.broadcasted_iota(jnp.int32, (owners, width), 0)
    elem_at = lax.broadcasted_iota(jnp.int32, (elems, width), 0)
    sums = jnp.zeros((3 * owners, elems), jnp.float32)
    for row in range(rows_x):
        local = ids_ref[row : row + 1, :] - first_element
        owner = lax.shift_right_logical(local, 7)
        inside = jnp.bitwise_and(local, elems - 1)
        split = jnp.where(owner_at == owner, terms[row : row + 1, :], 0.0)
        pieces = [piece.astype(jnp.float32) for piece in thirds(split)]
        left = jnp.concatenate(pieces, axis=0).astype(jnp.bfloat16)
        sums = sums + lax.dot_general(
            left, one_hot(elem_at == inside), NT, preferred_element_type=jnp.float32
        )
    elem_ref[...] = sums[:owners] + sums[owners : 2 * owners] + sums[2 * owners :]


def solve(place, own, low, high, left, right, mid, side, ids, epochs, grp_count, tile_count):
    rows_x, rows_y = ids.shape
    height = rows_x + 2 * REACH
    elems = LANES
    tall = 8 * height
    spec = pl.BlockSpec(memory_space=pltpu.VMEM)
    f32 = jnp.float32
    return pl.pallas_call(
        lambda *refs: solve_kernel(epochs, grp_count, tile_count, *refs),
        in_specs=[pl.BlockSpec(memory_space=pltpu.SMEM)] + [spec] * 8,
        out_specs=(spec, spec),
        out_shape=(
            jax.ShapeDtypeStruct((2, rows_x, rows_y), f32),
            jax.ShapeDtypeStruct((tile_count * rows_x * rows_y // 128 // elems, elems), f32),
        ),
        scratch_shapes=[
            pltpu.VMEM((FIELDS, tall, LANES), f32),
            pltpu.VMEM((5, 8 * (rows_x + 2 * STRIP), LANES), f32),
            pltpu.VMEM((PICARD, tall, LANES), f32),
            pltpu.VMEM((PICARD, tall, LANES), f32),
            pltpu.VMEM((PICARD, tall, LANES), f32),
            pltpu.VMEM((PICARD, tall, LANES), f32),
            pltpu.VMEM((PICARD, 2, tall, LANES), f32),
            pltpu.VMEM((tall, LANES), f32),
            pltpu.VMEM((2, tall, LANES), f32),
            pltpu.VMEM((2, tall, LANES), f32),
            pltpu.VMEM((PICARD * SWEEPS, 2, 8 * rows_x, LANES), f32),
            pltpu.VMEM((2, 8 * rows_x, LANES), f32),
            pltpu.VMEM((8 * rows_x, LANES), f32),
            pltpu.VMEM((rows_x, rows_y), f32),
        ],
        compiler_params=pltpu.CompilerParams(vmem_limit_bytes=VMEM_BYTES),
        cost_estimate=pl.CostEstimate(
            flops=80_000_000, bytes_accessed=4_000_000, transcendentals=0
        ),
        name="solve",
    )(place, own, low, high, left, right, mid, side, ids)


def sum_onto_owner(terms, axis):
    count = lax.axis_size(axis)
    me = lax.axis_index(axis)
    span = 1
    terms = terms.reshape((count, 1, -1))
    while span < count:
        halves = terms.reshape((terms.shape[0] // 2, 2, -1))
        bit = me // span % 2
        mine = lax.dynamic_index_in_dim(halves, bit, 1, keepdims=False)
        other = lax.dynamic_index_in_dim(halves, 1 - bit, 1, keepdims=False)
        terms = mine + lax.ppermute(other, axis, [(i, i ^ span) for i in range(count)])
        span *= 2
    return terms.reshape(-1)


def shards(
    start_velocity,
    driving_stress,
    viscosity,
    friction,
    cell_element,
    observed,
    look,
    row_owner,
    row_cell,
):
    rows_x, rows_y = friction.shape
    row_dev, epochs = observed.shape
    groups, tiles = lax.axis_size("grp"), lax.axis_size("tile")
    devices = groups * tiles
    cap = max(2, 2 * row_dev // devices)
    own = jnp.concatenate([start_velocity, driving_stress, viscosity, friction[None]], axis=0)
    low, high = halo_pair(own, "grp")
    outgoing = pack_rows(groups, tiles, look, observed, row_owner, row_cell)
    arrived = lax.all_to_all(outgoing, ("grp", "tile"), split_axis=0, concat_axis=0, tiled=True)
    to_low, to_high = edges(low, own, high)
    count = tiles
    forward = [(i, i + 1) for i in range(count - 1)]
    backward = [(target, source) for source, target in forward]
    left = lax.ppermute(to_high, "tile", forward)
    right = lax.ppermute(to_low, "tile", backward)
    mid, side = add_on_nodes(arrived, cap, rows_x, rows_y)
    place = jnp.stack([lax.axis_index("grp"), lax.axis_index("tile")]).astype(jnp.int32)
    stress_adjoint, terms = solve(
        place, own, low, high, left, right, mid, side, cell_element, epochs, groups, tiles
    )
    return stress_adjoint, sum_onto_owner(terms, "tile")


def solution(mesh):
    return jax.shard_map(
        shards,
        mesh=mesh,
        in_specs=(
            P(None, "grp", "tile"),
            P(None, "grp", "tile"),
            P(None, "grp", "tile"),
            P("grp", "tile"),
            P("grp", "tile"),
            P(("grp", "tile"), None),
            P(None, ("grp", "tile"), None),
            P(("grp", "tile"), None),
            P(("grp", "tile")),
        ),
        out_specs=(P(None, "grp", "tile"), P(("grp", "tile"))),
        check_vma=False,
    )
```

```python
import math

import jax
import jax.numpy as jnp
from jax import lax
from jax.experimental import pallas as pl
from jax.experimental.pallas import tpu as pltpu
from jax.sharding import PartitionSpec as P

SWEEPS = 8
PICARD = 2
LANES = 128
FIELDS = 7
REACH = 32
CHUNK = 64
CHUNKS = 8
DELAY = 8
STRIP = 16
VMEM_BYTES = 60 * 1024 * 1024
NT = (((1,), (1,)), ((), ()))


def halo_pair(block, axis):
    count = lax.axis_size(axis)
    forward = [(i, i + 1) for i in range(count - 1)]
    backward = [(target, source) for source, target in forward]
    return lax.ppermute(block, axis, forward), lax.ppermute(block, axis, backward)


def thirds(values):
    first = values.astype(jnp.bfloat16)
    rest = values - first.astype(jnp.float32)
    second = rest.astype(jnp.bfloat16)
    third = (rest - second.astype(jnp.float32)).astype(jnp.bfloat16)
    return first, second, third


def one_hot(mask):
    return jnp.where(mask, 1.0, 0.0).astype(jnp.bfloat16)


def rows_kernel(groups, tiles, cap, look_ref, obs_ref, owner_ref, cell_ref, out_ref, pad_ref):
    rows = obs_ref.shape[0]
    devices = groups * tiles
    look_x, look_y, obs = look_ref[0], look_ref[1], obs_ref[...]
    lane = lax.broadcasted_iota(jnp.int32, (rows, LANES), 1)
    sums = jnp.zeros((rows, LANES), jnp.float32)
    for place, (a, b) in enumerate(
        ((look_x, look_x), (look_x, look_y), (look_y, look_y), (look_x, obs), (look_y, obs))
    ):
        sums = jnp.where(lane == place, jnp.sum(a * b, axis=1, keepdims=True), sums)
    sums = sums.T[:8]
    owner = owner_ref[...]
    cell = cell_ref[...]
    named = lax.broadcasted_iota(jnp.int32, (devices, rows), 0) == owner
    before = lax.broadcasted_iota(jnp.int32, (rows, rows), 0) < lax.broadcasted_iota(
        jnp.int32, (rows, rows), 1
    )
    ranks = jnp.dot(one_hot(named), one_hot(before), preferred_element_type=jnp.float32)
    rank = jnp.sum(jnp.where(named, ranks, 0.0), axis=0, keepdims=True)
    slot = owner * cap + rank.astype(jnp.int32)
    hit = one_hot(lax.broadcasted_iota(jnp.int32, (devices * cap, rows), 0) == slot)
    cells = jnp.concatenate(
        [
            lax.shift_right_logical(cell, 7),
            jnp.bitwise_and(cell, 127),
            jnp.zeros((6, rows), jnp.int32),
        ],
        axis=0,
    ).astype(jnp.float32)
    s0, s1, s2 = thirds(sums)
    left = jnp.concatenate(
        [s0.astype(jnp.float32), s1.astype(jnp.float32), s2.astype(jnp.float32), cells], axis=0
    ).astype(jnp.bfloat16)
    placed = lax.dot_general(left, hit, NT, preferred_element_type=jnp.float32)
    table = placed[:8] + placed[8:16] + placed[16:24]
    row = lax.broadcasted_iota(jnp.int32, table.shape, 0)
    table = jnp.where(row == 5, placed[24:25] * 128.0 + placed[25:26], table)
    edge = jnp.zeros((8, LANES), jnp.float32)
    pad_ref[:, :LANES] = edge
    pad_ref[:, LANES : LANES + devices * cap] = table
    pad_ref[:, LANES + devices * cap :] = edge
    lane8 = lax.broadcasted_iota(jnp.int32, (8, LANES), 1)
    for g in range(groups):
        for t in range(tiles):
            start = (g * tiles + t - 1) * cap + LANES
            base, off = start // LANES * LANES, start % LANES
            piece = pad_ref[:, base : base + LANES]
            if off:
                after = pad_ref[:, base + LANES : base + 2 * LANES]
                piece = jnp.where(
                    lane8 < LANES - off,
                    pltpu.roll(piece, LANES - off, 1),
                    pltpu.roll(after, LANES - off, 1),
                )
            low = cap if t == 0 else 0
            high = 2 * cap if t == tiles - 1 else 3 * cap
            piece = jnp.where((lane8 >= low) & (lane8 < high), piece, 0.0)
            for d in range(3):
                goal = g - (d - 1)
                if 0 <= goal < groups:
                    out_ref[goal * tiles + t, d * 8 : d * 8 + 8, :] = piece
    for t in range(tiles):
        out_ref[t, 0:8, :] = edge
        out_ref[(groups - 1) * tiles + t, 16:24, :] = edge


def pack_rows(groups, tiles, look, observed, row_owner, row_cell):
    rows = observed.shape[0]
    devices = groups * tiles
    cap = max(2, 2 * rows // devices)
    return pl.pallas_call(
        lambda *refs: rows_kernel(groups, tiles, cap, *refs),
        out_shape=jax.ShapeDtypeStruct((devices, 24, LANES), jnp.float32),
        scratch_shapes=[pltpu.VMEM((8, devices * cap + 2 * LANES), jnp.float32)],
        compiler_params=pltpu.CompilerParams(vmem_limit_bytes=VMEM_BYTES),
        cost_estimate=pl.CostEstimate(flops=4_000_000, bytes_accessed=4_000_000, transcendentals=0),
        name="row_sums",
    )(look, observed, row_owner.reshape(1, rows), row_cell.reshape(1, rows))


def nodes_kernel(cap, rows_x, rows_y, in_ref, mid_ref, side_ref, left_ref, right_ref):
    devices = in_ref.shape[0]
    per = LANES // cap
    slots = devices * cap
    shift = rows_y.bit_length() - 1
    lane8 = lax.broadcasted_iota(jnp.int32, (8, LANES), 1)
    for d in range(3):
        wide = rows_x if d == 1 else STRIP
        first_x = {0: rows_x - STRIP, 1: 0, 2: 0}[d]
        out_x = {0: 0, 1: STRIP, 2: STRIP + rows_x}[d]
        lists = []
        for dt in range(3):
            parts = []
            for j in range(devices // per):
                part = jnp.zeros((8, LANES), jnp.float32)
                for q in range(per):
                    source = in_ref[j * per + q, d * 8 : d * 8 + 8, :]
                    turn = (q - dt) * cap % LANES
                    moved = pltpu.roll(source, turn, 1) if turn else source
                    part = jnp.where((lane8 >= q * cap) & (lane8 < q * cap + cap), moved, part)
                parts.append(part)
            lists.append(jnp.concatenate(parts, axis=1))
        for where, out_ref, width in (((1,), mid_ref, rows_y), ((0, 2), side_ref, LANES)):
            for position, dt in enumerate(where):
                values = lists[dt]
                cell = values[5:6].astype(jnp.int32)
                cell_x = lax.shift_right_logical(cell, shift) - first_x
                cell_y = jnp.bitwise_and(cell, rows_y - 1)
                begin = position * slots
                in_x = lax.broadcasted_iota(jnp.int32, (wide, slots), 0) == cell_x
                pieces = thirds(values)
                for p in range(3):
                    piece = pieces[p].astype(jnp.float32)
                    for f in range(5):
                        at = (p * 5 + f) * wide
                        left_ref[at : at + wide, begin : begin + slots] = jnp.where(
                            in_x, piece[f : f + 1], 0.0
                        ).astype(jnp.bfloat16)
                if dt == 0:
                    cell_y = cell_y - (rows_y - LANES)
                    cell_y = jnp.where(cell_y >= LANES - STRIP, cell_y, -1)
                if dt == 2:
                    cell_y = jnp.where(cell_y < STRIP, cell_y, -1)
                right_ref[:width, begin : begin + slots] = one_hot(
                    lax.broadcasted_iota(jnp.int32, (width, slots), 0) == cell_y
                )
            total = len(where) * slots
            added = lax.dot_general(
                left_ref[: 15 * wide, :total],
                right_ref[:width, :total],
                NT,
                preferred_element_type=jnp.float32,
            )
            added = added[: 5 * wide] + added[5 * wide : 10 * wide] + added[10 * wide :]
            for f in range(5):
                out_ref[f, out_x : out_x + wide, :] = added[f * wide : (f + 1) * wide]


def add_on_nodes(arrived, cap, rows_x, rows_y):
    slots = arrived.shape[0] * cap
    high = rows_x + 2 * STRIP
    return pl.pallas_call(
        lambda *refs: nodes_kernel(cap, rows_x, rows_y, *refs),
        out_shape=(
            jax.ShapeDtypeStruct((5, high, rows_y), jnp.float32),
            jax.ShapeDtypeStruct((5, high, LANES), jnp.float32),
        ),
        scratch_shapes=[
            pltpu.VMEM((15 * rows_x, 2 * slots), jnp.bfloat16),
            pltpu.VMEM((rows_y, 2 * slots), jnp.bfloat16),
        ],
        compiler_params=pltpu.CompilerParams(vmem_limit_bytes=VMEM_BYTES),
        cost_estimate=pl.CostEstimate(flops=4_000_000, bytes_accessed=4_000_000, transcendentals=0),
        name="add_on_nodes",
    )(arrived)


def edges_kernel(low_ref, own_ref, high_ref, to_low_ref, to_high_ref):
    lane = lax.broadcasted_iota(jnp.int32, (8, LANES), 1)
    last = own_ref.shape[2] - LANES
    sources = (low_ref, own_ref, high_ref)
    for f in range(FIELDS):
        for b in range(3):
            begin = jnp.zeros((8, LANES), jnp.float32)
            end = jnp.zeros((8, LANES), jnp.float32)
            for k in range(4):
                block = 3 * k + b
                ref, at = sources[block // 4], block % 4 * 8
                mine = (lane >= 32 * k) & (lane < 32 * k + 32)
                head = ref[f, at : at + 8, :LANES]
                tail = ref[f, at : at + 8, last:]
                if k:
                    head = pltpu.roll(head, 32 * k, 1)
                if k != 3:
                    tail = pltpu.roll(tail, 32 * k + 32, 1)
                begin = jnp.where(mine, head, begin)
                end = jnp.where(mine, tail, end)
            to_low_ref[f, b * 8 : b * 8 + 8, :] = begin
            to_high_ref[f, b * 8 : b * 8 + 8, :] = end


def edges(low, own, high):
    shape = jax.ShapeDtypeStruct((FIELDS, 24, LANES), jnp.float32)
    return pl.pallas_call(
        edges_kernel,
        out_shape=(shape, shape),
        compiler_params=pltpu.CompilerParams(vmem_limit_bytes=VMEM_BYTES),
        cost_estimate=pl.CostEstimate(flops=500_000, bytes_accessed=500_000, transcendentals=0),
        name="edges",
    )(low, own, high)


def tile_rows(row, count=1):
    return slice(8 * row, 8 * (row + count))


def to_rows(pieces, left, right, store):
    lane = lax.broadcasted_iota(jnp.int32, (8, LANES), 1)
    by_32 = [left] + [pltpu.roll(p, 32, 1) for p in pieces]
    by_96 = [pltpu.roll(p, 96, 1) for p in pieces] + [right]
    for k in range(4):
        store(2 * k, jnp.where(lane < 32, by_32[k], by_32[k + 1]))
        store(2 * k + 1, jnp.where(lane < 96, by_96[k], by_96[k + 1]))


def from_rows(load):
    lane = lax.broadcasted_iota(jnp.int32, (8, LANES), 1)
    return [
        jnp.where(lane < CHUNK, pltpu.roll(load(2 * k), 96, 1), pltpu.roll(load(2 * k + 1), 32, 1))
        for k in range(4)
    ]


def stencil_rows(load_u, load_v, visc, first_row, last_row, finish):
    ahead = {}
    waiting = []

    def issue(row):
        if row <= last_row + 1:
            ahead[row] = (
                pltpu.roll(load_u(row), LANES - 1, 1),
                pltpu.roll(load_v(row), LANES - 1, 1),
            )

    def lateral(row):
        u, v = load_u(row), load_v(row)
        u_next, v_next = ahead.pop(row)
        return u + u_next, u_next - u, v + v_next, v_next - v

    def stresses(row, here, after):
        half, quarter = visc(row)
        x_u, y_u = after[0] - here[0], after[1] + here[1]
        x_v, y_v = after[2] - here[2], after[3] + here[3]
        both = x_u + y_v
        return half * (x_u + both), half * (y_v + both), quarter * (y_u + x_v)

    def flush():
        row, turned_first, still_first, turned_second, still_second = waiting.pop(0)
        finish(row, load_u(row), load_v(row), turned_first + still_first, turned_second + still_second)

    for row in range(first_row - 1, first_row + 1 + DELAY):
        issue(row)
    before = lateral(first_row - 1)
    here = lateral(first_row)
    below = stresses(first_row - 1, before, here)
    for row in range(first_row, last_row + 1):
        issue(row + 1 + DELAY)
        after = lateral(row + 1)
        above = stresses(row, here, after)
        a, c = below[0] - above[0], below[1] + above[1]
        b, e = below[2] + above[2], below[2] - above[2]
        waiting.append((row, pltpu.roll(a + b, 1, 1), a - b, pltpu.roll(c + e, 1, 1), e - c))
        if len(waiting) > DELAY:
            flush()
        here, below = after, above
    while waiting:
        flush()


def solve_kernel(
    epochs,
    grp_count,
    tile_count,
    place_ref,
    own_ref,
    low_ref,
    high_ref,
    left_ref,
    right_ref,
    mid_ref,
    side_ref,
    ids_ref,
    out_ref,
    elem_ref,
    field,
    misfit,
    half_q,
    quarter_q,
    keep,
    prec,
    push,
    turn,
    wave_a,
    wave_b,
    seen,
    total,
    fric,
    terms,
):
    rows_x = own_ref.shape[1]
    height = rows_x + 2 * REACH
    grp, tile = place_ref[0], place_ref[1]

    sources = (low_ref, own_ref, high_ref)
    for f in range(FIELDS):
        for block in range(height // 8):
            ref, at = sources[block // 4], block % 4 * 8
            k, b = block // 3, block % 3
            left = left_ref[f, b * 8 : b * 8 + 8, :]
            right = right_ref[f, b * 8 : b * 8 + 8, :]
            if k:
                left = pltpu.roll(left, LANES - 32 * k, 1)
            if k != 3:
                right = pltpu.roll(right, 96 - 32 * k, 1)

            def store(s, value, f=f, block=block):
                field[f, pl.ds(64 * block + s, 8, stride=8), :] = value

            to_rows([ref[f, at : at + 8, LANES * j : LANES * j + LANES] for j in range(4)], left, right, store)
    for f in range(5):
        for block in range((rows_x + 2 * STRIP) // 8):
            at = block * 8
            beyond = side_ref[f, at : at + 8, :]

            def store(s, value, f=f, block=block):
                misfit[f, pl.ds(64 * block + s, 8, stride=8), :] = value

            to_rows(
                [mid_ref[f, at : at + 8, LANES * j : LANES * j + LANES] for j in range(4)],
                pltpu.roll(beyond, 32, 1),
                pltpu.roll(beyond, 96, 1),
                store,
            )

    lane = lax.broadcasted_iota(jnp.int32, (8, LANES), 1)
    chunk = lax.broadcasted_iota(jnp.int32, (8, LANES), 0)
    y = tile * (CHUNK * CHUNKS) + chunk * CHUNK + lane - 32
    in_y = (y >= 0) & (y < tile_count * (CHUNK * CHUNKS))
    in_low = in_y & jnp.broadcast_to(grp > 0, in_y.shape)
    in_high = in_y & jnp.broadcast_to(grp < grp_count - 1, in_y.shape)
    for p, (first_row, last_row) in enumerate(((2, height - 3), (2 + SWEEPS, height - 3 - SWEEPS))):

        def summed(row, p=p):
            e = field[4 + p, tile_rows(row), :]
            return e + pltpu.roll(e, LANES - 1, 1)

        before = summed(first_row - 1)
        row_sum = summed(first_row)
        quad = before + row_sum
        half_q[p, tile_rows(first_row - 1), :] = 0.125 * quad
        quarter_q[p, tile_rows(first_row - 1), :] = 0.0625 * quad
        quad_below = quad + pltpu.roll(quad, 1, 1)
        for row in range(first_row, last_row + 1):
            next_sum = summed(row + 1)
            quad = row_sum + next_sum
            half_q[p, tile_rows(row), :] = 0.125 * quad
            quarter_q[p, tile_rows(row), :] = 0.0625 * quad
            quad_above = quad + pltpu.roll(quad, 1, 1)
            fr = field[6, tile_rows(row), :]
            diagonal = (1.25 * 0.25) * (quad_below + quad_above) + fr
            inside = in_low if row < REACH else in_high if row >= REACH + rows_x else in_y
            pre = jnp.where(inside, 0.45 / diagonal, 0.0)
            prec[p, tile_rows(row), :] = pre
            keep[p, tile_rows(row), :] = 1.0 - pre * fr
            push[p, 0, tile_rows(row), :] = pre * field[2, tile_rows(row), :]
            push[p, 1, tile_rows(row), :] = pre * field[3, tile_rows(row), :]
            if p == 0:
                turn[tile_rows(row), :] = pre * (1.0 / 0.45)
            else:
                turn[tile_rows(row), :] = turn[tile_rows(row), :] * diagonal
            row_sum, quad_below = next_sum, quad_above

    def visc(p):
        return lambda row: (half_q[p, tile_rows(row), :], quarter_q[p, tile_rows(row), :])

    def forward(p, step, source, target, first_row, last_row):
        def finish(row, u, v, first, second):
            at = tile_rows(row)
            pre, rest = prec[p, at, :], keep[p, at, :]
            new_u = rest * u + push[p, 0, at, :] - pre * first
            new_v = rest * v + push[p, 1, at, :] - pre * second
            target(0, row, new_u)
            target(1, row, new_v)
            if REACH <= row < REACH + rows_x:
                here = pl.ds(8 * (row - REACH), 8)
                seen[step, 0, here, :] = u + (new_u - u) * (1.0 / 0.45)
                seen[step, 1, here, :] = v + (new_v - v) * (1.0 / 0.45)

        stencil_rows(lambda r: source(0, r), lambda r: source(1, r), visc(p), first_row, last_row, finish)

    def reader(ref):
        return lambda c, row: ref[c, tile_rows(row), :]

    def writer(ref):
        def write(c, row, value):
            ref[c, tile_rows(row), :] = value

        return write

    for c in range(2):
        wave_a[c] = field[c]
    for p in range(PICARD):
        rows = (2 + SWEEPS * p, height - 3 - SWEEPS * p)

        def pair(i, _, p=p, rows=rows):
            forward(p, SWEEPS * p + 2 * i, reader(wave_a), writer(wave_b), *rows)
            forward(p, SWEEPS * p + 2 * i + 1, reader(wave_b), writer(wave_a), *rows)
            return 0

        lax.fori_loop(0, SWEEPS // 2, pair, 0)

    first_row, last_row = 17, height - 18
    for row in range(first_row, last_row + 1):
        at, mis = tile_rows(row), tile_rows(row - (REACH - STRIP))
        u, v = wave_a[0, at, :], wave_a[1, at, :]
        cross = misfit[1, mis, :]
        scale = prec[1, at, :] * (1.0 / math.sqrt(epochs))
        wave_a[0, at, :] = scale * (misfit[0, mis, :] * u + cross * v - misfit[3, mis, :])
        wave_a[1, at, :] = scale * (cross * u + misfit[2, mis, :] * v - misfit[4, mis, :])
    total[...] = jnp.zeros_like(total)
    fric[...] = jnp.zeros_like(fric)

    def gather(step, source):
        for row in range(REACH, REACH + rows_x):
            here = tile_rows(row - REACH)
            u, v = source(0, row), source(1, row)
            total[0, here, :] = total[0, here, :] + u
            total[1, here, :] = total[1, here, :] + v
            fric[here, :] = fric[here, :] - (u * seen[step, 0, here, :] + v * seen[step, 1, here, :])

    def backward(p, step, source, target, first_row, last_row, switch=False):
        def finish(row, u, v, first, second):
            at = tile_rows(row)
            pre, rest = prec[p, at, :], keep[p, at, :]
            new_u, new_v = rest * u - pre * first, rest * v - pre * second
            if switch:
                new_u, new_v = new_u * turn[at, :], new_v * turn[at, :]
            target(0, row, new_u)
            target(1, row, new_v)
            if REACH <= row < REACH + rows_x:
                here = tile_rows(row - REACH)
                total[0, here, :] = total[0, here, :] + u
                total[1, here, :] = total[1, here, :] + v
                fric[here, :] = fric[here, :] - (u * seen[step, 0, here, :] + v * seen[step, 1, here, :])

        stencil_rows(lambda r: source(0, r), lambda r: source(1, r), visc(p), first_row, last_row, finish)

    for p in range(PICARD - 1, -1, -1):
        edge = 18 if p == PICARD - 1 else 18 + SWEEPS
        rows = (edge, height - 1 - edge)
        top = SWEEPS * (p + 1) - 1

        def pair(i, _, p=p, rows=rows, top=top):
            backward(p, top - 2 * i, reader(wave_a), writer(wave_b), *rows)
            backward(p, top - 2 * i - 1, reader(wave_b), writer(wave_a), *rows)
            return 0

        lax.fori_loop(0, SWEEPS // 2 - 1, pair, 0)
        backward(p, top - SWEEPS + 2, reader(wave_a), writer(wave_b), *rows)
        if p:
            backward(p, top - SWEEPS + 1, reader(wave_b), writer(wave_a), *rows, switch=True)
        else:
            gather(0, reader(wave_b))

    for block in range(rows_x // 8):
        at = slice(block * 8, block * 8 + 8)
        for c in range(2):
            tiles = from_rows(lambda s: total[c, pl.ds(64 * block + s, 8, stride=8), :])
            for k in range(4):
                out_ref[c, at, LANES * k : LANES * k + LANES] = tiles[k]
        tiles = from_rows(lambda s: fric[pl.ds(64 * block + s, 8, stride=8), :])
        for k in range(4):
            terms[at, LANES * k : LANES * k + LANES] = (
                tiles[k] * own_ref[6, at, LANES * k : LANES * k + LANES]
            )

    owners, elems = elem_ref.shape
    first_element = grp * (owners * elems)
    width = ids_ref.shape[1]
    owner_at = lax.broadcasted_iota(jnp.int32, (owners, width), 0)
    elem_at = lax.broadcasted_iota(jnp.int32, (elems, width), 0)
    sums = jnp.zeros((3 * owners, elems), jnp.float32)
    for row in range(rows_x):
        local = ids_ref[row : row + 1, :] - first_element
        owner = lax.shift_right_logical(local, 7)
        inside = jnp.bitwise_and(local, elems - 1)
        split = jnp.where(owner_at == owner, terms[row : row + 1, :], 0.0)
        pieces = [piece.astype(jnp.float32) for piece in thirds(split)]
        left = jnp.concatenate(pieces, axis=0).astype(jnp.bfloat16)
        sums = sums + lax.dot_general(
            left, one_hot(elem_at == inside), NT, preferred_element_type=jnp.float32
        )
    elem_ref[...] = sums[:owners] + sums[owners : 2 * owners] + sums[2 * owners :]


def solve(place, own, low, high, left, right, mid, side, ids, epochs, grp_count, tile_count):
    rows_x, rows_y = ids.shape
    height = rows_x + 2 * REACH
    elems = LANES
    tall = 8 * height
    spec = pl.BlockSpec(memory_space=pltpu.VMEM)
    f32 = jnp.float32
    return pl.pallas_call(
        lambda *refs: solve_kernel(epochs, grp_count, tile_count, *refs),
        in_specs=[pl.BlockSpec(memory_space=pltpu.SMEM)] + [spec] * 8,
        out_specs=(spec, spec),
        out_shape=(
            jax.ShapeDtypeStruct((2, rows_x, rows_y), f32),
            jax.ShapeDtypeStruct((tile_count * rows_x * rows_y // 128 // elems, elems), f32),
        ),
        scratch_shapes=[
            pltpu.VMEM((FIELDS, tall, LANES), f32),
            pltpu.VMEM((5, 8 * (rows_x + 2 * STRIP), LANES), f32),
            pltpu.VMEM((PICARD, tall, LANES), f32),
            pltpu.VMEM((PICARD, tall, LANES), f32),
            pltpu.VMEM((PICARD, tall, LANES), f32),
            pltpu.VMEM((PICARD, tall, LANES), f32),
            pltpu.VMEM((PICARD, 2, tall, LANES), f32),
            pltpu.VMEM((tall, LANES), f32),
            pltpu.VMEM((2, tall, LANES), f32),
            pltpu.VMEM((2, tall, LANES), f32),
            pltpu.VMEM((PICARD * SWEEPS, 2, 8 * rows_x, LANES), f32),
            pltpu.VMEM((2, 8 * rows_x, LANES), f32),
            pltpu.VMEM((8 * rows_x, LANES), f32),
            pltpu.VMEM((rows_x, rows_y), f32),
        ],
        compiler_params=pltpu.CompilerParams(vmem_limit_bytes=VMEM_BYTES),
        cost_estimate=pl.CostEstimate(
            flops=80_000_000, bytes_accessed=4_000_000, transcendentals=0
        ),
        name="solve",
    )(place, own, low, high, left, right, mid, side, ids)


def sum_onto_owner(terms, axis):
    count = lax.axis_size(axis)
    me = lax.axis_index(axis)
    span = 1
    terms = terms.reshape((count, 1, -1))
    while span < count:
        halves = terms.reshape((terms.shape[0] // 2, 2, -1))
        bit = me // span % 2
        mine = lax.dynamic_index_in_dim(halves, bit, 1, keepdims=False)
        other = lax.dynamic_index_in_dim(halves, 1 - bit, 1, keepdims=False)
        terms = mine + lax.ppermute(other, axis, [(i, i ^ span) for i in range(count)])
        span *= 2
    return terms.reshape(-1)


def shards(
    start_velocity,
    driving_stress,
    viscosity,
    friction,
    cell_element,
    observed,
    look,
    row_owner,
    row_cell,
):
    rows_x, rows_y = friction.shape
    row_dev, epochs = observed.shape
    groups, tiles = lax.axis_size("grp"), lax.axis_size("tile")
    devices = groups * tiles
    cap = max(2, 2 * row_dev // devices)
    own = jnp.concatenate([start_velocity, driving_stress, viscosity, friction[None]], axis=0)
    low, high = halo_pair(own, "grp")
    outgoing = pack_rows(groups, tiles, look, observed, row_owner, row_cell)
    arrived = lax.all_to_all(outgoing, ("grp", "tile"), split_axis=0, concat_axis=0, tiled=True)
    to_low, to_high = edges(low, own, high)
    count = tiles
    forward = [(i, i + 1) for i in range(count - 1)]
    backward = [(target, source) for source, target in forward]
    left = lax.ppermute(to_high, "tile", forward)
    right = lax.ppermute(to_low, "tile", backward)
    mid, side = add_on_nodes(arrived, cap, rows_x, rows_y)
    place = jnp.stack([lax.axis_index("grp"), lax.axis_index("tile")]).astype(jnp.int32)
    stress_adjoint, terms = solve(
        place, own, low, high, left, right, mid, side, cell_element, epochs, groups, tiles
    )
    return stress_adjoint, sum_onto_owner(terms, "tile")


def solution(mesh):
    return jax.shard_map(
        shards,
        mesh=mesh,
        in_specs=(
            P(None, "grp", "tile"),
            P(None, "grp", "tile"),
            P(None, "grp", "tile"),
            P("grp", "tile"),
            P("grp", "tile"),
            P(("grp", "tile"), None),
            P(None, ("grp", "tile"), None),
            P(("grp", "tile"), None),
            P(("grp", "tile")),
        ),
        out_specs=(P(None, "grp", "tile"), P(("grp", "tile"))),
        check_vma=False,
    )
```

```python
import math

import jax
import jax.numpy as jnp
from jax import lax
from jax.experimental import pallas as pl
from jax.experimental.pallas import tpu as pltpu
from jax.sharding import PartitionSpec as P

SWEEPS = 8
PICARD = 2
LANES = 128
FIELDS = 7
REACH = 32
CHUNK = 64
CHUNKS = 8
DELAY = 14
STRIP = 16
MIB = 1024 * 1024
NT = (((1,), (1,)), ((), ()))


def halo_pair(block, axis):
    count = lax.axis_size(axis)
    forward = [(i, i + 1) for i in range(count - 1)]
    backward = [(target, source) for source, target in forward]
    return lax.ppermute(block, axis, forward), lax.ppermute(block, axis, backward)


def thirds(values):
    first = values.astype(jnp.bfloat16)
    rest = values - first.astype(jnp.float32)
    second = rest.astype(jnp.bfloat16)
    third = (rest - second.astype(jnp.float32)).astype(jnp.bfloat16)
    return first, second, third


def one_hot(mask):
    return jnp.where(mask, 1.0, 0.0).astype(jnp.bfloat16)


def rows_kernel(groups, tiles, cap, look_ref, obs_ref, owner_ref, cell_ref, out_ref, pad_ref):
    rows = obs_ref.shape[0]
    devices = groups * tiles
    look_x, look_y, obs = look_ref[0], look_ref[1], obs_ref[...]
    lane = lax.broadcasted_iota(jnp.int32, (rows, LANES), 1)
    sums = jnp.zeros((rows, LANES), jnp.float32)
    for place, (a, b) in enumerate(
        ((look_x, look_x), (look_x, look_y), (look_y, look_y), (look_x, obs), (look_y, obs))
    ):
        sums = jnp.where(lane == place, jnp.sum(a * b, axis=1, keepdims=True), sums)
    sums = sums.T[:8]
    owner = owner_ref[...]
    cell = cell_ref[...]
    named = lax.broadcasted_iota(jnp.int32, (devices, rows), 0) == owner
    before = lax.broadcasted_iota(jnp.int32, (rows, rows), 0) < lax.broadcasted_iota(
        jnp.int32, (rows, rows), 1
    )
    ranks = jnp.dot(one_hot(named), one_hot(before), preferred_element_type=jnp.float32)
    rank = jnp.sum(jnp.where(named, ranks, 0.0), axis=0, keepdims=True)
    slot = owner * cap + rank.astype(jnp.int32)
    hit = one_hot(lax.broadcasted_iota(jnp.int32, (devices * cap, rows), 0) == slot)
    cells = jnp.concatenate(
        [
            lax.shift_right_logical(cell, 7),
            jnp.bitwise_and(cell, 127),
            jnp.zeros((6, rows), jnp.int32),
        ],
        axis=0,
    ).astype(jnp.float32)
    s0, s1, s2 = thirds(sums)
    left = jnp.concatenate(
        [s0.astype(jnp.float32), s1.astype(jnp.float32), s2.astype(jnp.float32), cells], axis=0
    ).astype(jnp.bfloat16)
    placed = lax.dot_general(left, hit, NT, preferred_element_type=jnp.float32)
    table = placed[:8] + placed[8:16] + placed[16:24]
    row = lax.broadcasted_iota(jnp.int32, table.shape, 0)
    table = jnp.where(row == 5, placed[24:25] * 128.0 + placed[25:26], table)
    edge = jnp.zeros((8, LANES), jnp.float32)
    pad_ref[:, :LANES] = edge
    pad_ref[:, LANES : LANES + devices * cap] = table
    pad_ref[:, LANES + devices * cap :] = edge
    lane8 = lax.broadcasted_iota(jnp.int32, (8, LANES), 1)
    for g in range(groups):
        for t in range(tiles):
            start = (g * tiles + t - 1) * cap + LANES
            base, off = start // LANES * LANES, start % LANES
            piece = pad_ref[:, base : base + LANES]
            if off:
                after = pad_ref[:, base + LANES : base + 2 * LANES]
                piece = jnp.where(
                    lane8 < LANES - off,
                    pltpu.roll(piece, LANES - off, 1),
                    pltpu.roll(after, LANES - off, 1),
                )
            low = cap if t == 0 else 0
            high = 2 * cap if t == tiles - 1 else 3 * cap
            piece = jnp.where((lane8 >= low) & (lane8 < high), piece, 0.0)
            for d in range(3):
                goal = g - (d - 1)
                if 0 <= goal < groups:
                    out_ref[goal * tiles + t, d * 8 : d * 8 + 8, :] = piece
    for t in range(tiles):
        out_ref[t, 0:8, :] = edge
        out_ref[(groups - 1) * tiles + t, 16:24, :] = edge


def pack_rows(groups, tiles, look, observed, row_owner, row_cell):
    rows = observed.shape[0]
    devices = groups * tiles
    cap = max(2, 2 * rows // devices)
    return pl.pallas_call(
        lambda *refs: rows_kernel(groups, tiles, cap, *refs),
        out_shape=jax.ShapeDtypeStruct((devices, 24, LANES), jnp.float32),
        scratch_shapes=[pltpu.VMEM((8, devices * cap + 2 * LANES), jnp.float32)],
        compiler_params=pltpu.CompilerParams(vmem_limit_bytes=12 * MIB),
        cost_estimate=pl.CostEstimate(flops=4_000_000, bytes_accessed=80_000_000, transcendentals=0),
        name="row_sums",
    )(look, observed, row_owner.reshape(1, rows), row_cell.reshape(1, rows))


def nodes_kernel(cap, rows_x, rows_y, in_ref, mid_ref, side_ref, left_ref, right_ref):
    devices = in_ref.shape[0]
    per = LANES // cap
    slots = devices * cap
    shift = rows_y.bit_length() - 1
    lane8 = lax.broadcasted_iota(jnp.int32, (8, LANES), 1)
    for d in range(3):
        wide = rows_x if d == 1 else STRIP
        first_x = {0: rows_x - STRIP, 1: 0, 2: 0}[d]
        out_x = {0: 0, 1: STRIP, 2: STRIP + rows_x}[d]
        lists = []
        for dt in range(3):
            parts = []
            for j in range(devices // per):
                part = jnp.zeros((8, LANES), jnp.float32)
                for q in range(per):
                    source = in_ref[j * per + q, d * 8 : d * 8 + 8, :]
                    turn = (q - dt) * cap % LANES
                    moved = pltpu.roll(source, turn, 1) if turn else source
                    part = jnp.where((lane8 >= q * cap) & (lane8 < q * cap + cap), moved, part)
                parts.append(part)
            lists.append(jnp.concatenate(parts, axis=1))
        for where, out_ref, width in (((1,), mid_ref, rows_y), ((0, 2), side_ref, LANES)):
            for position, dt in enumerate(where):
                values = lists[dt]
                cell = values[5:6].astype(jnp.int32)
                cell_x = lax.shift_right_logical(cell, shift) - first_x
                cell_y = jnp.bitwise_and(cell, rows_y - 1)
                begin = position * slots
                in_x = lax.broadcasted_iota(jnp.int32, (wide, slots), 0) == cell_x
                pieces = thirds(values)
                for p in range(3):
                    piece = pieces[p].astype(jnp.float32)
                    for f in range(5):
                        at = (p * 5 + f) * wide
                        left_ref[at : at + wide, begin : begin + slots] = jnp.where(
                            in_x, piece[f : f + 1], 0.0
                        ).astype(jnp.bfloat16)
                if dt == 0:
                    cell_y = cell_y - (rows_y - LANES)
                    cell_y = jnp.where(cell_y >= LANES - STRIP, cell_y, -1)
                if dt == 2:
                    cell_y = jnp.where(cell_y < STRIP, cell_y, -1)
                right_ref[:width, begin : begin + slots] = one_hot(
                    lax.broadcasted_iota(jnp.int32, (width, slots), 0) == cell_y
                )
            total = len(where) * slots
            added = lax.dot_general(
                left_ref[: 15 * wide, :total],
                right_ref[:width, :total],
                NT,
                preferred_element_type=jnp.float32,
            )
            added = added[: 5 * wide] + added[5 * wide : 10 * wide] + added[10 * wide :]
            for f in range(5):
                out_ref[f, out_x : out_x + wide, :] = added[f * wide : (f + 1) * wide]


def add_on_nodes(arrived, cap, rows_x, rows_y):
    slots = arrived.shape[0] * cap
    high = rows_x + 2 * STRIP
    return pl.pallas_call(
        lambda *refs: nodes_kernel(cap, rows_x, rows_y, *refs),
        out_shape=(
            jax.ShapeDtypeStruct((5, high, rows_y), jnp.float32),
            jax.ShapeDtypeStruct((5, high, LANES), jnp.float32),
        ),
        scratch_shapes=[
            pltpu.VMEM((15 * rows_x, 2 * slots), jnp.bfloat16),
            pltpu.VMEM((rows_y, 2 * slots), jnp.bfloat16),
        ],
        compiler_params=pltpu.CompilerParams(vmem_limit_bytes=16 * MIB),
        cost_estimate=pl.CostEstimate(flops=4_000_000, bytes_accessed=4_000_000, transcendentals=0),
        name="add_on_nodes",
    )(arrived)


def edges_kernel(*refs):
    heads, tails, (to_low_ref, to_high_ref) = refs[:3], refs[3:6], refs[6:]
    lane = lax.broadcasted_iota(jnp.int32, (8, LANES), 1)
    for f in range(FIELDS):
        for b in range(3):
            begin = jnp.zeros((8, LANES), jnp.float32)
            end = jnp.zeros((8, LANES), jnp.float32)
            for k in range(4):
                block = 3 * k + b
                at = block % 4 * 8
                mine = (lane >= 32 * k) & (lane < 32 * k + 32)
                head, tail = heads[block // 4][f, at : at + 8, :], tails[block // 4][f, at : at + 8, :]
                if k:
                    head = pltpu.roll(head, 32 * k, 1)
                if k != 3:
                    tail = pltpu.roll(tail, 32 * k + 32, 1)
                begin = jnp.where(mine, head, begin)
                end = jnp.where(mine, tail, end)
            to_low_ref[f, b * 8 : b * 8 + 8, :] = begin
            to_high_ref[f, b * 8 : b * 8 + 8, :] = end


def edges(low, own, high):
    shape = jax.ShapeDtypeStruct((FIELDS, 24, LANES), jnp.float32)
    part = (FIELDS, own.shape[1], LANES)
    last = own.shape[2] // LANES - 1
    head = pl.BlockSpec(part, lambda i: (0, 0, 0))
    tail = pl.BlockSpec(part, lambda i: (0, 0, last))
    whole = pl.BlockSpec(shape.shape, lambda i: (0, 0, 0))
    return pl.pallas_call(
        edges_kernel,
        grid=(1,),
        in_specs=[head] * 3 + [tail] * 3,
        out_specs=(whole, whole),
        out_shape=(shape, shape),
        compiler_params=pltpu.CompilerParams(vmem_limit_bytes=4 * MIB),
        cost_estimate=pl.CostEstimate(flops=100_000_000_000, bytes_accessed=500_000, transcendentals=0),
        name="edges",
    )(low, own, high, low, own, high)


def tile_rows(row, count=1):
    return slice(8 * row, 8 * (row + count))


def to_rows(pieces, left, right, store):
    lane = lax.broadcasted_iota(jnp.int32, (8, LANES), 1)
    by_32 = [left] + [pltpu.roll(p, 32, 1) for p in pieces]
    by_96 = [pltpu.roll(p, 96, 1) for p in pieces] + [right]
    for k in range(4):
        store(2 * k, jnp.where(lane < 32, by_32[k], by_32[k + 1]))
        store(2 * k + 1, jnp.where(lane < 96, by_96[k], by_96[k + 1]))


def from_rows(load):
    lane = lax.broadcasted_iota(jnp.int32, (8, LANES), 1)
    return [
        jnp.where(lane < CHUNK, pltpu.roll(load(2 * k), 96, 1), pltpu.roll(load(2 * k + 1), 32, 1))
        for k in range(4)
    ]


def stencil_rows(load_u, load_v, visc, first_row, last_row, finish):
    ahead = {}
    waiting = []

    def issue(row):
        if row <= last_row + 1:
            ahead[row] = (
                pltpu.roll(load_u(row), LANES - 1, 1),
                pltpu.roll(load_v(row), LANES - 1, 1),
            )

    def lateral(row):
        u, v = load_u(row), load_v(row)
        u_next, v_next = ahead.pop(row)
        return u + u_next, u_next - u, v + v_next, v_next - v

    def stresses(row, here, after):
        half, quarter = visc(row)
        x_u, y_u = after[0] - here[0], after[1] + here[1]
        x_v, y_v = after[2] - here[2], after[3] + here[3]
        both = x_u + y_v
        return half * (x_u + both), half * (y_v + both), quarter * (y_u + x_v)

    def flush():
        row, turned_first, still_first, turned_second, still_second = waiting.pop(0)
        finish(row, load_u(row), load_v(row), turned_first + still_first, turned_second + still_second)

    for row in range(first_row - 1, first_row + 1 + DELAY):
        issue(row)
    before = lateral(first_row - 1)
    here = lateral(first_row)
    below = stresses(first_row - 1, before, here)
    for row in range(first_row, last_row + 1):
        issue(row + 1 + DELAY)
        after = lateral(row + 1)
        above = stresses(row, here, after)
        a, c = below[0] - above[0], below[1] + above[1]
        b, e = below[2] + above[2], below[2] - above[2]
        waiting.append((row, pltpu.roll(a + b, 1, 1), a - b, pltpu.roll(c + e, 1, 1), e - c))
        if len(waiting) > DELAY:
            flush()
        here, below = after, above
    while waiting:
        flush()


def solve_kernel(
    epochs,
    grp_count,
    tile_count,
    place_ref,
    own_ref,
    low_ref,
    high_ref,
    left_ref,
    right_ref,
    mid_ref,
    side_ref,
    ids_ref,
    out_ref,
    elem_ref,
    field,
    misfit,
    half_q,
    quarter_q,
    keep,
    prec,
    push,
    turn,
    wave_a,
    wave_b,
    seen,
    total,
    fric,
    terms,
):
    rows_x = own_ref.shape[1]
    height = rows_x + 2 * REACH
    grp, tile = place_ref[0], place_ref[1]

    sources = (low_ref, own_ref, high_ref)
    for f in range(FIELDS):
        for block in range(height // 8):
            ref, at = sources[block // 4], block % 4 * 8
            k, b = block // 3, block % 3
            left = left_ref[f, b * 8 : b * 8 + 8, :]
            right = right_ref[f, b * 8 : b * 8 + 8, :]
            if k:
                left = pltpu.roll(left, LANES - 32 * k, 1)
            if k != 3:
                right = pltpu.roll(right, 96 - 32 * k, 1)

            def store(s, value, f=f, block=block):
                field[f, pl.ds(64 * block + s, 8, stride=8), :] = value

            to_rows([ref[f, at : at + 8, LANES * j : LANES * j + LANES] for j in range(4)], left, right, store)
    for f in range(5):
        for block in range((rows_x + 2 * STRIP) // 8):
            at = block * 8
            beyond = side_ref[f, at : at + 8, :]

            def store(s, value, f=f, block=block):
                misfit[f, pl.ds(64 * block + s, 8, stride=8), :] = value

            to_rows(
                [mid_ref[f, at : at + 8, LANES * j : LANES * j + LANES] for j in range(4)],
                pltpu.roll(beyond, 32, 1),
                pltpu.roll(beyond, 96, 1),
                store,
            )

    lane = lax.broadcasted_iota(jnp.int32, (8, LANES), 1)
    chunk = lax.broadcasted_iota(jnp.int32, (8, LANES), 0)
    y = tile * (CHUNK * CHUNKS) + chunk * CHUNK + lane - 32
    in_y = (y >= 0) & (y < tile_count * (CHUNK * CHUNKS))
    in_low = in_y & jnp.broadcast_to(grp > 0, in_y.shape)
    in_high = in_y & jnp.broadcast_to(grp < grp_count - 1, in_y.shape)
    for p, (first_row, last_row) in enumerate(((2, height - 3), (2 + SWEEPS, height - 3 - SWEEPS))):

        def summed(row, p=p):
            e = field[4 + p, tile_rows(row), :]
            return e + pltpu.roll(e, LANES - 1, 1)

        before = summed(first_row - 1)
        row_sum = summed(first_row)
        quad = before + row_sum
        half_q[p, tile_rows(first_row - 1), :] = 0.125 * quad
        quarter_q[p, tile_rows(first_row - 1), :] = 0.0625 * quad
        quad_below = quad + pltpu.roll(quad, 1, 1)
        for row in range(first_row, last_row + 1):
            next_sum = summed(row + 1)
            quad = row_sum + next_sum
            half_q[p, tile_rows(row), :] = 0.125 * quad
            quarter_q[p, tile_rows(row), :] = 0.0625 * quad
            quad_above = quad + pltpu.roll(quad, 1, 1)
            fr = field[6, tile_rows(row), :]
            diagonal = (1.25 * 0.25) * (quad_below + quad_above) + fr
            inside = in_low if row < REACH else in_high if row >= REACH + rows_x else in_y
            pre = jnp.where(inside, 0.45 / diagonal, 0.0)
            prec[p, tile_rows(row), :] = pre
            keep[p, tile_rows(row), :] = 1.0 - pre * fr
            push[p, 0, tile_rows(row), :] = pre * field[2, tile_rows(row), :]
            push[p, 1, tile_rows(row), :] = pre * field[3, tile_rows(row), :]
            if p == 0:
                turn[tile_rows(row), :] = pre * (1.0 / 0.45)
            else:
                turn[tile_rows(row), :] = turn[tile_rows(row), :] * diagonal
            row_sum, quad_below = next_sum, quad_above

    def visc(p):
        return lambda row: (half_q[p, tile_rows(row), :], quarter_q[p, tile_rows(row), :])

    def forward(p, step, source, target, first_row, last_row):
        def finish(row, u, v, first, second):
            at = tile_rows(row)
            pre, rest = prec[p, at, :], keep[p, at, :]
            new_u = rest * u + push[p, 0, at, :] - pre * first
            new_v = rest * v + push[p, 1, at, :] - pre * second
            target(0, row, new_u)
            target(1, row, new_v)
            if REACH <= row < REACH + rows_x:
                here = pl.ds(8 * (row - REACH), 8)
                seen[step, 0, here, :] = u + (new_u - u) * (1.0 / 0.45)
                seen[step, 1, here, :] = v + (new_v - v) * (1.0 / 0.45)

        stencil_rows(lambda r: source(0, r), lambda r: source(1, r), visc(p), first_row, last_row, finish)

    def reader(ref):
        return lambda c, row: ref[c, tile_rows(row), :]

    def writer(ref):
        def write(c, row, value):
            ref[c, tile_rows(row), :] = value

        return write

    for c in range(2):
        wave_a[c] = field[c]
    for p in range(PICARD):
        rows = (2 + SWEEPS * p, height - 3 - SWEEPS * p)

        def pair(i, _, p=p, rows=rows):
            forward(p, SWEEPS * p + 2 * i, reader(wave_a), writer(wave_b), *rows)
            forward(p, SWEEPS * p + 2 * i + 1, reader(wave_b), writer(wave_a), *rows)
            return 0

        lax.fori_loop(0, SWEEPS // 2, pair, 0)

    first_row, last_row = 17, height - 18
    for row in range(first_row, last_row + 1):
        at, mis = tile_rows(row), tile_rows(row - (REACH - STRIP))
        u, v = wave_a[0, at, :], wave_a[1, at, :]
        cross = misfit[1, mis, :]
        scale = prec[1, at, :] * (1.0 / math.sqrt(epochs))
        wave_a[0, at, :] = scale * (misfit[0, mis, :] * u + cross * v - misfit[3, mis, :])
        wave_a[1, at, :] = scale * (cross * u + misfit[2, mis, :] * v - misfit[4, mis, :])
    total[...] = jnp.zeros_like(total)
    fric[...] = jnp.zeros_like(fric)

    def gather(step, source):
        for row in range(REACH, REACH + rows_x):
            here = tile_rows(row - REACH)
            u, v = source(0, row), source(1, row)
            total[0, here, :] = total[0, here, :] + u
            total[1, here, :] = total[1, here, :] + v
            fric[here, :] = fric[here, :] - (u * seen[step, 0, here, :] + v * seen[step, 1, here, :])

    def backward(p, step, source, target, first_row, last_row, switch=False):
        def finish(row, u, v, first, second):
            at = tile_rows(row)
            pre, rest = prec[p, at, :], keep[p, at, :]
            new_u, new_v = rest * u - pre * first, rest * v - pre * second
            if switch:
                new_u, new_v = new_u * turn[at, :], new_v * turn[at, :]
            target(0, row, new_u)
            target(1, row, new_v)
            if REACH <= row < REACH + rows_x:
                here = tile_rows(row - REACH)
                total[0, here, :] = total[0, here, :] + u
                total[1, here, :] = total[1, here, :] + v
                fric[here, :] = fric[here, :] - (u * seen[step, 0, here, :] + v * seen[step, 1, here, :])

        stencil_rows(lambda r: source(0, r), lambda r: source(1, r), visc(p), first_row, last_row, finish)

    for p in range(PICARD - 1, -1, -1):
        edge = 18 if p == PICARD - 1 else 18 + SWEEPS
        rows = (edge, height - 1 - edge)
        top = SWEEPS * (p + 1) - 1

        def pair(i, _, p=p, rows=rows, top=top):
            backward(p, top - 2 * i, reader(wave_a), writer(wave_b), *rows)
            backward(p, top - 2 * i - 1, reader(wave_b), writer(wave_a), *rows)
            return 0

        lax.fori_loop(0, SWEEPS // 2 - 1, pair, 0)
        backward(p, top - SWEEPS + 2, reader(wave_a), writer(wave_b), *rows)
        if p:
            backward(p, top - SWEEPS + 1, reader(wave_b), writer(wave_a), *rows, switch=True)
        else:
            gather(0, reader(wave_b))

    for block in range(rows_x // 8):
        at = slice(block * 8, block * 8 + 8)
        for c in range(2):
            tiles = from_rows(lambda s: total[c, pl.ds(64 * block + s, 8, stride=8), :])
            for k in range(4):
                out_ref[c, at, LANES * k : LANES * k + LANES] = tiles[k]
        tiles = from_rows(lambda s: fric[pl.ds(64 * block + s, 8, stride=8), :])
        for k in range(4):
            terms[at, LANES * k : LANES * k + LANES] = (
                tiles[k] * own_ref[6, at, LANES * k : LANES * k + LANES]
            )

    owners, elems = elem_ref.shape
    first_element = grp * (owners * elems)
    width = ids_ref.shape[1]
    owner_at = lax.broadcasted_iota(jnp.int32, (owners, width), 0)
    elem_at = lax.broadcasted_iota(jnp.int32, (elems, width), 0)
    sums = jnp.zeros((3 * owners, elems), jnp.float32)
    for row in range(rows_x):
        local = ids_ref[row : row + 1, :] - first_element
        owner = lax.shift_right_logical(local, 7)
        inside = jnp.bitwise_and(local, elems - 1)
        split = jnp.where(owner_at == owner, terms[row : row + 1, :], 0.0)
        pieces = [piece.astype(jnp.float32) for piece in thirds(split)]
        left = jnp.concatenate(pieces, axis=0).astype(jnp.bfloat16)
        sums = sums + lax.dot_general(
            left, one_hot(elem_at == inside), NT, preferred_element_type=jnp.float32
        )
    elem_ref[...] = sums[:owners] + sums[owners : 2 * owners] + sums[2 * owners :]


def solve(place, own, low, high, left, right, mid, side, ids, epochs, grp_count, tile_count):
    rows_x, rows_y = ids.shape
    height = rows_x + 2 * REACH
    elems = LANES
    tall = 8 * height
    spec = pl.BlockSpec(memory_space=pltpu.VMEM)
    f32 = jnp.float32
    return pl.pallas_call(
        lambda *refs: solve_kernel(epochs, grp_count, tile_count, *refs),
        in_specs=[pl.BlockSpec(memory_space=pltpu.SMEM)] + [spec] * 8,
        out_specs=(spec, spec),
        out_shape=(
            jax.ShapeDtypeStruct((2, rows_x, rows_y), f32),
            jax.ShapeDtypeStruct((tile_count * rows_x * rows_y // 128 // elems, elems), f32),
        ),
        scratch_shapes=[
            pltpu.VMEM((FIELDS, tall, LANES), f32),
            pltpu.VMEM((5, 8 * (rows_x + 2 * STRIP), LANES), f32),
            pltpu.VMEM((PICARD, tall, LANES), f32),
            pltpu.VMEM((PICARD, tall, LANES), f32),
            pltpu.VMEM((PICARD, tall, LANES), f32),
            pltpu.VMEM((PICARD, tall, LANES), f32),
            pltpu.VMEM((PICARD, 2, tall, LANES), f32),
            pltpu.VMEM((tall, LANES), f32),
            pltpu.VMEM((2, tall, LANES), f32),
            pltpu.VMEM((2, tall, LANES), f32),
            pltpu.VMEM((PICARD * SWEEPS, 2, 8 * rows_x, LANES), f32),
            pltpu.VMEM((2, 8 * rows_x, LANES), f32),
            pltpu.VMEM((8 * rows_x, LANES), f32),
            pltpu.VMEM((rows_x, rows_y), f32),
        ],
        compiler_params=pltpu.CompilerParams(vmem_limit_bytes=28 * MIB),
        cost_estimate=pl.CostEstimate(
            flops=80_000_000, bytes_accessed=4_000_000, transcendentals=0
        ),
        name="solve",
    )(place, own, low, high, left, right, mid, side, ids)


def sum_onto_owner(terms, axis):
    count = lax.axis_size(axis)
    me = lax.axis_index(axis)
    span = 1
    terms = terms.reshape((count, 1, -1))
    while span < count:
        halves = terms.reshape((terms.shape[0] // 2, 2, -1))
        bit = me // span % 2
        mine = lax.dynamic_index_in_dim(halves, bit, 1, keepdims=False)
        other = lax.dynamic_index_in_dim(halves, 1 - bit, 1, keepdims=False)
        terms = mine + lax.ppermute(other, axis, [(i, i ^ span) for i in range(count)])
        span *= 2
    return terms.reshape(-1)


def shards(
    start_velocity,
    driving_stress,
    viscosity,
    friction,
    cell_element,
    observed,
    look,
    row_owner,
    row_cell,
):
    rows_x, rows_y = friction.shape
    row_dev, epochs = observed.shape
    groups, tiles = lax.axis_size("grp"), lax.axis_size("tile")
    devices = groups * tiles
    cap = max(2, 2 * row_dev // devices)
    own = jnp.concatenate([start_velocity, driving_stress, viscosity, friction[None]], axis=0)
    low, high = halo_pair(own, "grp")
    outgoing = pack_rows(groups, tiles, look, observed, row_owner, row_cell)
    arrived = lax.all_to_all(outgoing, ("grp", "tile"), split_axis=0, concat_axis=0, tiled=True)
    to_low, to_high = edges(low, own, high)
    count = tiles
    forward = [(i, i + 1) for i in range(count - 1)]
    backward = [(target, source) for source, target in forward]
    left = lax.ppermute(to_high, "tile", forward)
    right = lax.ppermute(to_low, "tile", backward)
    mid, side = add_on_nodes(arrived, cap, rows_x, rows_y)
    place = jnp.stack([lax.axis_index("grp"), lax.axis_index("tile")]).astype(jnp.int32)
    stress_adjoint, terms = solve(
        place, own, low, high, left, right, mid, side, cell_element, epochs, groups, tiles
    )
    return stress_adjoint, sum_onto_owner(terms, "tile")


def solution(mesh):
    return jax.shard_map(
        shards,
        mesh=mesh,
        in_specs=(
            P(None, "grp", "tile"),
            P(None, "grp", "tile"),
            P(None, "grp", "tile"),
            P("grp", "tile"),
            P("grp", "tile"),
            P(("grp", "tile"), None),
            P(None, ("grp", "tile"), None),
            P(("grp", "tile"), None),
            P(("grp", "tile")),
        ),
        out_specs=(P(None, "grp", "tile"), P(("grp", "tile"))),
        check_vma=False,
    )
```

```python
import math

import jax
import jax.numpy as jnp
from jax import lax
from jax.experimental import pallas as pl
from jax.experimental.pallas import tpu as pltpu
from jax.sharding import PartitionSpec as P

SWEEPS = 8
PICARD = 2
LANES = 128
FIELDS = 7
REACH = 32
CHUNK = 64
CHUNKS = 8
DELAY = 14
STRIP = 16
MIB = 1024 * 1024
NT = (((1,), (1,)), ((), ()))


def swap_pairs(block, axis, first):
    pairs = [(i, i + 1) for i in range(first, lax.axis_size(axis) - 1, 2)]
    return lax.ppermute(block, axis, pairs + [(b, a) for a, b in pairs])


def thirds(values):
    first = values.astype(jnp.bfloat16)
    rest = values - first.astype(jnp.float32)
    second = rest.astype(jnp.bfloat16)
    third = (rest - second.astype(jnp.float32)).astype(jnp.bfloat16)
    return first, second, third


def one_hot(mask):
    return jnp.where(mask, 1.0, 0.0).astype(jnp.bfloat16)


def rows_kernel(groups, tiles, cap, look_ref, obs_ref, owner_ref, cell_ref, out_ref, pad_ref):
    rows = obs_ref.shape[0]
    devices = groups * tiles
    look_x, look_y, obs = look_ref[0], look_ref[1], obs_ref[...]
    lane = lax.broadcasted_iota(jnp.int32, (rows, LANES), 1)
    sums = jnp.zeros((rows, LANES), jnp.float32)
    for place, (a, b) in enumerate(
        ((look_x, look_x), (look_x, look_y), (look_y, look_y), (look_x, obs), (look_y, obs))
    ):
        sums = jnp.where(lane == place, jnp.sum(a * b, axis=1, keepdims=True), sums)
    sums = sums.T[:8]
    owner = owner_ref[...]
    cell = cell_ref[...]
    named = lax.broadcasted_iota(jnp.int32, (devices, rows), 0) == owner
    before = lax.broadcasted_iota(jnp.int32, (rows, rows), 0) < lax.broadcasted_iota(
        jnp.int32, (rows, rows), 1
    )
    ranks = jnp.dot(one_hot(named), one_hot(before), preferred_element_type=jnp.float32)
    rank = jnp.sum(jnp.where(named, ranks, 0.0), axis=0, keepdims=True)
    slot = owner * cap + rank.astype(jnp.int32)
    hit = one_hot(lax.broadcasted_iota(jnp.int32, (devices * cap, rows), 0) == slot)
    cells = jnp.concatenate(
        [
            lax.shift_right_logical(cell, 7),
            jnp.bitwise_and(cell, 127),
            jnp.zeros((6, rows), jnp.int32),
        ],
        axis=0,
    ).astype(jnp.float32)
    s0, s1, s2 = thirds(sums)
    left = jnp.concatenate(
        [s0.astype(jnp.float32), s1.astype(jnp.float32), s2.astype(jnp.float32), cells], axis=0
    ).astype(jnp.bfloat16)
    placed = lax.dot_general(left, hit, NT, preferred_element_type=jnp.float32)
    table = placed[:8] + placed[8:16] + placed[16:24]
    row = lax.broadcasted_iota(jnp.int32, table.shape, 0)
    table = jnp.where(row == 5, placed[24:25] * 128.0 + placed[25:26], table)
    edge = jnp.zeros((8, LANES), jnp.float32)
    pad_ref[:, :LANES] = edge
    pad_ref[:, LANES : LANES + devices * cap] = table
    pad_ref[:, LANES + devices * cap :] = edge
    lane8 = lax.broadcasted_iota(jnp.int32, (8, LANES), 1)
    row8 = lax.broadcasted_iota(jnp.int32, (8, LANES), 0)
    tail = (lane8 >= 3 * cap) & (lane8 < 4 * cap) & (row8 < 6)
    packed = tail | (row8 >= 6)
    pieces = {}
    for g in range(groups):
        for t in range(tiles):
            start = (g * tiles + t - 1) * cap + LANES
            base, off = start // LANES * LANES, start % LANES
            piece = pad_ref[:, base : base + LANES]
            if off:
                after = pad_ref[:, base + LANES : base + 2 * LANES]
                piece = jnp.where(
                    lane8 < LANES - off,
                    pltpu.roll(piece, LANES - off, 1),
                    pltpu.roll(after, LANES - off, 1),
                )
            low = cap if t == 0 else 0
            high = 2 * cap if t == tiles - 1 else 3 * cap
            piece = jnp.where((lane8 >= low) & (lane8 < high), piece, 0.0)
            turned = jnp.where(row8 < 6, pltpu.roll(piece, 3 * cap, 1), 0.0)
            shared = jnp.where(row8 < 6, pltpu.roll(piece, 2 * cap, 1), 0.0)
            for f in range(6):
                spread = jnp.broadcast_to(piece[f : f + 1], (8, LANES))
                spread = pltpu.roll(spread, (f % 4 - 2) * cap % LANES, 1) if f % 4 != 2 else spread
                group = (lane8 >= f % 4 * cap) & (lane8 < f % 4 * cap + cap) & (row8 == 6 + f // 4)
                turned = jnp.where(group, spread, turned)
            pieces[g, t] = piece, turned, shared
    for g in range(groups):
        for t in range(tiles):
            top = pieces[g - 1, t][0] if g else edge
            low = pieces[g, t][0]
            if g < groups - 1:
                _, turned, shared = pieces[g + 1, t]
                top = jnp.where(packed, turned, top)
                low = jnp.where(tail, shared, low)
            out_ref[g * tiles + t, 0:8, :] = top
            out_ref[g * tiles + t, 8:16, :] = low


def pack_rows(groups, tiles, look, observed, row_owner, row_cell):
    rows = observed.shape[0]
    devices = groups * tiles
    cap = max(2, 2 * rows // devices)
    return pl.pallas_call(
        lambda *refs: rows_kernel(groups, tiles, cap, *refs),
        out_shape=jax.ShapeDtypeStruct((devices, 16, LANES), jnp.float32),
        scratch_shapes=[pltpu.VMEM((8, devices * cap + 2 * LANES), jnp.float32)],
        compiler_params=pltpu.CompilerParams(vmem_limit_bytes=12 * MIB),
        cost_estimate=pl.CostEstimate(flops=4_000_000, bytes_accessed=80_000_000, transcendentals=0),
        name="row_sums",
    )(look, observed, row_owner.reshape(1, rows), row_cell.reshape(1, rows))


def nodes_kernel(cap, rows_x, rows_y, in_ref, mid_ref, side_ref, left_ref, right_ref):
    devices = in_ref.shape[0]
    per = LANES // cap
    slots = devices * cap
    shift = rows_y.bit_length() - 1
    lane8 = lax.broadcasted_iota(jnp.int32, (8, LANES), 1)
    row8 = lax.broadcasted_iota(jnp.int32, (8, LANES), 0)
    for d in range(3):
        wide = rows_x if d == 1 else STRIP
        first_x = {0: rows_x - STRIP, 1: 0, 2: 0}[d]
        out_x = {0: 0, 1: STRIP, 2: STRIP + rows_x}[d]
        lists = []
        for dt in range(3):
            parts = []
            for j in range(devices // per):
                part = jnp.zeros((8, LANES), jnp.float32)
                for q in range(per):
                    here = (lane8 >= q * cap) & (lane8 < q * cap + cap)
                    if d == 2 and dt == 2:
                        for f in range(6):
                            source = in_ref[j * per + q, 6 + f // 4 : 7 + f // 4, :]
                            moved = jnp.broadcast_to(source, (8, LANES))
                            turn = (q - f % 4) * cap % LANES
                            moved = pltpu.roll(moved, turn, 1) if turn else moved
                            part = jnp.where(here & (row8 == f), moved, part)
                        continue
                    at = 8 * dt if d == 2 else 8 * d
                    source = in_ref[j * per + q, at : at + 8, :]
                    turn = (q - (3 if d == 2 else dt)) * cap % LANES
                    moved = pltpu.roll(source, turn, 1) if turn else source
                    part = jnp.where(here & (row8 < 6), moved, part)
                parts.append(part)
            lists.append(jnp.concatenate(parts, axis=1))
        for where, out_ref, width in (((1,), mid_ref, rows_y), ((0, 2), side_ref, LANES)):
            for position, dt in enumerate(where):
                values = lists[dt]
                cell = values[5:6].astype(jnp.int32)
                cell_x = lax.shift_right_logical(cell, shift) - first_x
                cell_y = jnp.bitwise_and(cell, rows_y - 1)
                begin = position * slots
                in_x = lax.broadcasted_iota(jnp.int32, (wide, slots), 0) == cell_x
                pieces = thirds(values)
                for p in range(3):
                    piece = pieces[p].astype(jnp.float32)
                    for f in range(5):
                        at = (p * 5 + f) * wide
                        left_ref[at : at + wide, begin : begin + slots] = jnp.where(
                            in_x, piece[f : f + 1], 0.0
                        ).astype(jnp.bfloat16)
                if dt == 0:
                    cell_y = cell_y - (rows_y - LANES)
                    cell_y = jnp.where(cell_y >= LANES - STRIP, cell_y, -1)
                if dt == 2:
                    cell_y = jnp.where(cell_y < STRIP, cell_y, -1)
                right_ref[:width, begin : begin + slots] = one_hot(
                    lax.broadcasted_iota(jnp.int32, (width, slots), 0) == cell_y
                )
            total = len(where) * slots
            added = lax.dot_general(
                left_ref[: 15 * wide, :total],
                right_ref[:width, :total],
                NT,
                preferred_element_type=jnp.float32,
            )
            added = added[: 5 * wide] + added[5 * wide : 10 * wide] + added[10 * wide :]
            for f in range(5):
                out_ref[f, out_x : out_x + wide, :] = added[f * wide : (f + 1) * wide]


def add_on_nodes(arrived, cap, rows_x, rows_y):
    slots = arrived.shape[0] * cap
    high = rows_x + 2 * STRIP
    return pl.pallas_call(
        lambda *refs: nodes_kernel(cap, rows_x, rows_y, *refs),
        out_shape=(
            jax.ShapeDtypeStruct((5, high, rows_y), jnp.float32),
            jax.ShapeDtypeStruct((5, high, LANES), jnp.float32),
        ),
        scratch_shapes=[
            pltpu.VMEM((15 * rows_x, 2 * slots), jnp.bfloat16),
            pltpu.VMEM((rows_y, 2 * slots), jnp.bfloat16),
        ],
        compiler_params=pltpu.CompilerParams(vmem_limit_bytes=16 * MIB),
        cost_estimate=pl.CostEstimate(flops=4_000_000, bytes_accessed=4_000_000, transcendentals=0),
        name="add_on_nodes",
    )(arrived)


def edges_kernel(place_ref, *refs):
    heads, tails, (even_ref, odd_ref) = refs[:3], refs[3:6], refs[6:]
    lane = lax.broadcasted_iota(jnp.int32, (8, LANES), 1)
    odd_grp = jnp.broadcast_to(place_ref[0] % 2 == 1, lane.shape)
    odd_tile = jnp.broadcast_to(place_ref[1] % 2 == 1, lane.shape)

    def pick(parts, block, f):
        own, even, odd = [part[f, block % 4 * 8 : block % 4 * 8 + 8, :] for part in parts]
        return (jnp.where(odd_grp, even, odd), own, jnp.where(odd_grp, odd, even))[block // 4]

    for f in range(FIELDS):
        for b in range(3):
            begin = jnp.zeros((8, LANES), jnp.float32)
            end = jnp.zeros((8, LANES), jnp.float32)
            for k in range(4):
                block = 3 * k + b
                mine = (lane >= 32 * k) & (lane < 32 * k + 32)
                head, tail = pick(heads, block, f), pick(tails, block, f)
                if k:
                    head = pltpu.roll(head, 32 * k, 1)
                if k != 3:
                    tail = pltpu.roll(tail, 32 * k + 32, 1)
                begin = jnp.where(mine, head, begin)
                end = jnp.where(mine, tail, end)
            even_ref[f, b * 8 : b * 8 + 8, :] = jnp.where(odd_tile, begin, end)
            odd_ref[f, b * 8 : b * 8 + 8, :] = jnp.where(odd_tile, end, begin)


def edges(place, own, even, odd):
    shape = jax.ShapeDtypeStruct((FIELDS, 24, LANES), jnp.float32)
    part = (FIELDS, own.shape[1], LANES)
    last = own.shape[2] // LANES - 1
    head = pl.BlockSpec(part, lambda i: (0, 0, 0))
    tail = pl.BlockSpec(part, lambda i: (0, 0, last))
    whole = pl.BlockSpec(shape.shape, lambda i: (0, 0, 0))
    return pl.pallas_call(
        edges_kernel,
        grid=(1,),
        in_specs=[pl.BlockSpec(memory_space=pltpu.SMEM)] + [head] * 3 + [tail] * 3,
        out_specs=(whole, whole),
        out_shape=(shape, shape),
        compiler_params=pltpu.CompilerParams(vmem_limit_bytes=4 * MIB),
        cost_estimate=pl.CostEstimate(flops=100_000_000_000, bytes_accessed=500_000, transcendentals=0),
        name="edges",
    )(place, own, even, odd, own, even, odd)


def tile_rows(row, count=1):
    return slice(8 * row, 8 * (row + count))


def to_rows(pieces, left, right, store):
    lane = lax.broadcasted_iota(jnp.int32, (8, LANES), 1)
    by_32 = [left] + [pltpu.roll(p, 32, 1) for p in pieces]
    by_96 = [pltpu.roll(p, 96, 1) for p in pieces] + [right]
    for k in range(4):
        store(2 * k, jnp.where(lane < 32, by_32[k], by_32[k + 1]))
        store(2 * k + 1, jnp.where(lane < 96, by_96[k], by_96[k + 1]))


def from_rows(load):
    lane = lax.broadcasted_iota(jnp.int32, (8, LANES), 1)
    return [
        jnp.where(lane < CHUNK, pltpu.roll(load(2 * k), 96, 1), pltpu.roll(load(2 * k + 1), 32, 1))
        for k in range(4)
    ]


def stencil_rows(load_u, load_v, visc, first_row, last_row, finish):
    ahead = {}
    waiting = []

    def issue(row):
        if row <= last_row + 1:
            ahead[row] = (
                pltpu.roll(load_u(row), LANES - 1, 1),
                pltpu.roll(load_v(row), LANES - 1, 1),
            )

    def lateral(row):
        u, v = load_u(row), load_v(row)
        u_next, v_next = ahead.pop(row)
        return u + u_next, u_next - u, v + v_next, v_next - v

    def stresses(row, here, after):
        half, quarter = visc(row)
        x_u, y_u = after[0] - here[0], after[1] + here[1]
        x_v, y_v = after[2] - here[2], after[3] + here[3]
        both = x_u + y_v
        return half * (x_u + both), half * (y_v + both), quarter * (y_u + x_v)

    def flush():
        row, turned_first, still_first, turned_second, still_second = waiting.pop(0)
        finish(row, load_u(row), load_v(row), turned_first + still_first, turned_second + still_second)

    for row in range(first_row - 1, first_row + 1 + DELAY):
        issue(row)
    before = lateral(first_row - 1)
    here = lateral(first_row)
    below = stresses(first_row - 1, before, here)
    for row in range(first_row, last_row + 1):
        issue(row + 1 + DELAY)
        after = lateral(row + 1)
        above = stresses(row, here, after)
        a, c = below[0] - above[0], below[1] + above[1]
        b, e = below[2] + above[2], below[2] - above[2]
        waiting.append((row, pltpu.roll(a + b, 1, 1), a - b, pltpu.roll(c + e, 1, 1), e - c))
        if len(waiting) > DELAY:
            flush()
        here, below = after, above
    while waiting:
        flush()


def solve_kernel(
    epochs,
    grp_count,
    tile_count,
    place_ref,
    own_ref,
    grp_even_ref,
    grp_odd_ref,
    tile_even_ref,
    tile_odd_ref,
    mid_ref,
    side_ref,
    ids_ref,
    out_ref,
    elem_ref,
    field,
    misfit,
    half_q,
    quarter_q,
    keep,
    prec,
    push,
    turn,
    wave_a,
    wave_b,
    seen,
    total,
    fric,
    terms,
):
    rows_x = own_ref.shape[1]
    height = rows_x + 2 * REACH
    grp, tile = place_ref[0], place_ref[1]

    odd_grp = jnp.broadcast_to(grp % 2 == 1, (8, LANES))
    odd_tile = jnp.broadcast_to(tile % 2 == 1, (8, LANES))

    def pick(f, block, j):
        at = (f, slice(block % 4 * 8, block % 4 * 8 + 8), slice(LANES * j, LANES * j + LANES))
        if block // 4 == 1:
            return own_ref[at]
        even, odd = grp_even_ref[at], grp_odd_ref[at]
        return jnp.where(odd_grp, even, odd) if block < 4 else jnp.where(odd_grp, odd, even)

    for f in range(FIELDS):
        for block in range(height // 8):
            k, b = block // 3, block % 3
            even = tile_even_ref[f, b * 8 : b * 8 + 8, :]
            odd = tile_odd_ref[f, b * 8 : b * 8 + 8, :]
            left = jnp.where(odd_tile, even, odd)
            right = jnp.where(odd_tile, odd, even)
            if k:
                left = pltpu.roll(left, LANES - 32 * k, 1)
            if k != 3:
                right = pltpu.roll(right, 96 - 32 * k, 1)

            def store(s, value, f=f, block=block):
                field[f, pl.ds(64 * block + s, 8, stride=8), :] = value

            to_rows([pick(f, block, j) for j in range(4)], left, right, store)
    for f in range(5):
        for block in range((rows_x + 2 * STRIP) // 8):
            at = block * 8
            beyond = side_ref[f, at : at + 8, :]

            def store(s, value, f=f, block=block):
                misfit[f, pl.ds(64 * block + s, 8, stride=8), :] = value

            to_rows(
                [mid_ref[f, at : at + 8, LANES * j : LANES * j + LANES] for j in range(4)],
                pltpu.roll(beyond, 32, 1),
                pltpu.roll(beyond, 96, 1),
                store,
            )

    lane = lax.broadcasted_iota(jnp.int32, (8, LANES), 1)
    chunk = lax.broadcasted_iota(jnp.int32, (8, LANES), 0)
    y = tile * (CHUNK * CHUNKS) + chunk * CHUNK + lane - 32
    in_y = (y >= 0) & (y < tile_count * (CHUNK * CHUNKS))
    in_low = in_y & jnp.broadcast_to(grp > 0, in_y.shape)
    in_high = in_y & jnp.broadcast_to(grp < grp_count - 1, in_y.shape)
    for p, (first_row, last_row) in enumerate(((2, height - 3), (2 + SWEEPS, height - 3 - SWEEPS))):

        def summed(row, p=p):
            e = field[4 + p, tile_rows(row), :]
            return e + pltpu.roll(e, LANES - 1, 1)

        before = summed(first_row - 1)
        row_sum = summed(first_row)
        quad = before + row_sum
        half_q[p, tile_rows(first_row - 1), :] = 0.125 * quad
        quarter_q[p, tile_rows(first_row - 1), :] = 0.0625 * quad
        quad_below = quad + pltpu.roll(quad, 1, 1)
        for row in range(first_row, last_row + 1):
            next_sum = summed(row + 1)
            quad = row_sum + next_sum
            half_q[p, tile_rows(row), :] = 0.125 * quad
            quarter_q[p, tile_rows(row), :] = 0.0625 * quad
            quad_above = quad + pltpu.roll(quad, 1, 1)
            fr = field[6, tile_rows(row), :]
            diagonal = (1.25 * 0.25) * (quad_below + quad_above) + fr
            inside = in_low if row < REACH else in_high if row >= REACH + rows_x else in_y
            pre = jnp.where(inside, 0.45 / diagonal, 0.0)
            prec[p, tile_rows(row), :] = pre
            keep[p, tile_rows(row), :] = 1.0 - pre * fr
            push[p, 0, tile_rows(row), :] = pre * field[2, tile_rows(row), :]
            push[p, 1, tile_rows(row), :] = pre * field[3, tile_rows(row), :]
            if p == 0:
                turn[tile_rows(row), :] = pre * (1.0 / 0.45)
            else:
                turn[tile_rows(row), :] = turn[tile_rows(row), :] * diagonal
            row_sum, quad_below = next_sum, quad_above

    def visc(p):
        return lambda row: (half_q[p, tile_rows(row), :], quarter_q[p, tile_rows(row), :])

    def forward(p, step, source, target, first_row, last_row):
        def finish(row, u, v, first, second):
            at = tile_rows(row)
            pre, rest = prec[p, at, :], keep[p, at, :]
            new_u = rest * u + push[p, 0, at, :] - pre * first
            new_v = rest * v + push[p, 1, at, :] - pre * second
            target(0, row, new_u)
            target(1, row, new_v)
            if REACH <= row < REACH + rows_x:
                here = pl.ds(8 * (row - REACH), 8)
                seen[step, 0, here, :] = u + (new_u - u) * (1.0 / 0.45)
                seen[step, 1, here, :] = v + (new_v - v) * (1.0 / 0.45)

        stencil_rows(lambda r: source(0, r), lambda r: source(1, r), visc(p), first_row, last_row, finish)

    def reader(ref):
        return lambda c, row: ref[c, tile_rows(row), :]

    def writer(ref):
        def write(c, row, value):
            ref[c, tile_rows(row), :] = value

        return write

    for c in range(2):
        wave_a[c] = field[c]
    for p in range(PICARD):
        rows = (2 + SWEEPS * p, height - 3 - SWEEPS * p)

        def pair(i, _, p=p, rows=rows):
            forward(p, SWEEPS * p + 2 * i, reader(wave_a), writer(wave_b), *rows)
            forward(p, SWEEPS * p + 2 * i + 1, reader(wave_b), writer(wave_a), *rows)
            return 0

        lax.fori_loop(0, SWEEPS // 2, pair, 0)

    first_row, last_row = 17, height - 18
    for row in range(first_row, last_row + 1):
        at, mis = tile_rows(row), tile_rows(row - (REACH - STRIP))
        u, v = wave_a[0, at, :], wave_a[1, at, :]
        cross = misfit[1, mis, :]
        scale = prec[1, at, :] * (1.0 / math.sqrt(epochs))
        wave_a[0, at, :] = scale * (misfit[0, mis, :] * u + cross * v - misfit[3, mis, :])
        wave_a[1, at, :] = scale * (cross * u + misfit[2, mis, :] * v - misfit[4, mis, :])
    total[...] = jnp.zeros_like(total)
    fric[...] = jnp.zeros_like(fric)

    def gather(step, source):
        for row in range(REACH, REACH + rows_x):
            here = tile_rows(row - REACH)
            u, v = source(0, row), source(1, row)
            total[0, here, :] = total[0, here, :] + u
            total[1, here, :] = total[1, here, :] + v
            fric[here, :] = fric[here, :] - (u * seen[step, 0, here, :] + v * seen[step, 1, here, :])

    def backward(p, step, source, target, first_row, last_row, switch=False):
        def finish(row, u, v, first, second):
            at = tile_rows(row)
            pre, rest = prec[p, at, :], keep[p, at, :]
            new_u, new_v = rest * u - pre * first, rest * v - pre * second
            if switch:
                new_u, new_v = new_u * turn[at, :], new_v * turn[at, :]
            target(0, row, new_u)
            target(1, row, new_v)
            if REACH <= row < REACH + rows_x:
                here = tile_rows(row - REACH)
                total[0, here, :] = total[0, here, :] + u
                total[1, here, :] = total[1, here, :] + v
                fric[here, :] = fric[here, :] - (u * seen[step, 0, here, :] + v * seen[step, 1, here, :])

        stencil_rows(lambda r: source(0, r), lambda r: source(1, r), visc(p), first_row, last_row, finish)

    for p in range(PICARD - 1, -1, -1):
        edge = 18 if p == PICARD - 1 else 18 + SWEEPS
        rows = (edge, height - 1 - edge)
        top = SWEEPS * (p + 1) - 1

        def pair(i, _, p=p, rows=rows, top=top):
            backward(p, top - 2 * i, reader(wave_a), writer(wave_b), *rows)
            backward(p, top - 2 * i - 1, reader(wave_b), writer(wave_a), *rows)
            return 0

        lax.fori_loop(0, SWEEPS // 2 - 1, pair, 0)
        backward(p, top - SWEEPS + 2, reader(wave_a), writer(wave_b), *rows)
        if p:
            backward(p, top - SWEEPS + 1, reader(wave_b), writer(wave_a), *rows, switch=True)
        else:
            gather(0, reader(wave_b))

    for block in range(rows_x // 8):
        at = slice(block * 8, block * 8 + 8)
        for c in range(2):
            tiles = from_rows(lambda s: total[c, pl.ds(64 * block + s, 8, stride=8), :])
            for k in range(4):
                out_ref[c, at, LANES * k : LANES * k + LANES] = tiles[k]
        tiles = from_rows(lambda s: fric[pl.ds(64 * block + s, 8, stride=8), :])
        for k in range(4):
            terms[at, LANES * k : LANES * k + LANES] = (
                tiles[k] * own_ref[6, at, LANES * k : LANES * k + LANES]
            )

    owners, elems = elem_ref.shape
    first_element = grp * (owners * elems)
    width = ids_ref.shape[1]
    owner_at = lax.broadcasted_iota(jnp.int32, (owners, width), 0)
    elem_at = lax.broadcasted_iota(jnp.int32, (elems, width), 0)
    sums = jnp.zeros((3 * owners, elems), jnp.float32)
    for row in range(rows_x):
        local = ids_ref[row : row + 1, :] - first_element
        owner = lax.shift_right_logical(local, 7)
        inside = jnp.bitwise_and(local, elems - 1)
        split = jnp.where(owner_at == owner, terms[row : row + 1, :], 0.0)
        pieces = [piece.astype(jnp.float32) for piece in thirds(split)]
        left = jnp.concatenate(pieces, axis=0).astype(jnp.bfloat16)
        sums = sums + lax.dot_general(
            left, one_hot(elem_at == inside), NT, preferred_element_type=jnp.float32
        )
    elem_ref[...] = sums[:owners] + sums[owners : 2 * owners] + sums[2 * owners :]


def solve(place, own, grp_halos, tile_halos, mid, side, ids, epochs, grp_count, tile_count):
    rows_x, rows_y = ids.shape
    height = rows_x + 2 * REACH
    elems = LANES
    tall = 8 * height
    spec = pl.BlockSpec(memory_space=pltpu.VMEM)
    f32 = jnp.float32
    return pl.pallas_call(
        lambda *refs: solve_kernel(epochs, grp_count, tile_count, *refs),
        in_specs=[pl.BlockSpec(memory_space=pltpu.SMEM)] + [spec] * 8,
        out_specs=(spec, spec),
        out_shape=(
            jax.ShapeDtypeStruct((2, rows_x, rows_y), f32),
            jax.ShapeDtypeStruct((tile_count * rows_x * rows_y // 128 // elems, elems), f32),
        ),
        scratch_shapes=[
            pltpu.VMEM((FIELDS, tall, LANES), f32),
            pltpu.VMEM((5, 8 * (rows_x + 2 * STRIP), LANES), f32),
            pltpu.VMEM((PICARD, tall, LANES), f32),
            pltpu.VMEM((PICARD, tall, LANES), f32),
            pltpu.VMEM((PICARD, tall, LANES), f32),
            pltpu.VMEM((PICARD, tall, LANES), f32),
            pltpu.VMEM((PICARD, 2, tall, LANES), f32),
            pltpu.VMEM((tall, LANES), f32),
            pltpu.VMEM((2, tall, LANES), f32),
            pltpu.VMEM((2, tall, LANES), f32),
            pltpu.VMEM((PICARD * SWEEPS, 2, 8 * rows_x, LANES), f32),
            pltpu.VMEM((2, 8 * rows_x, LANES), f32),
            pltpu.VMEM((8 * rows_x, LANES), f32),
            pltpu.VMEM((rows_x, rows_y), f32),
        ],
        compiler_params=pltpu.CompilerParams(vmem_limit_bytes=28 * MIB),
        cost_estimate=pl.CostEstimate(
            flops=80_000_000, bytes_accessed=4_000_000, transcendentals=0
        ),
        name="solve",
    )(place, own, *grp_halos, *tile_halos, mid, side, ids)


def sum_onto_owner(terms, axis):
    count = lax.axis_size(axis)
    me = lax.axis_index(axis)
    span = 1
    terms = terms.reshape((count, 1, -1))
    while span < count:
        halves = terms.reshape((terms.shape[0] // 2, 2, -1))
        bit = me // span % 2
        mine = lax.dynamic_index_in_dim(halves, bit, 1, keepdims=False)
        other = lax.dynamic_index_in_dim(halves, 1 - bit, 1, keepdims=False)
        terms = mine + lax.ppermute(other, axis, [(i, i ^ span) for i in range(count)])
        span *= 2
    return terms.reshape(-1)


def shards(
    start_velocity,
    driving_stress,
    viscosity,
    friction,
    cell_element,
    observed,
    look,
    row_owner,
    row_cell,
):
    rows_x, rows_y = friction.shape
    row_dev, epochs = observed.shape
    groups, tiles = lax.axis_size("grp"), lax.axis_size("tile")
    devices = groups * tiles
    cap = max(2, 2 * row_dev // devices)
    own = jnp.concatenate([start_velocity, driving_stress, viscosity, friction[None]], axis=0)
    place = jnp.stack([lax.axis_index("grp"), lax.axis_index("tile")]).astype(jnp.int32)
    grp_halos = [swap_pairs(own, "grp", first) for first in (0, 1)]
    outgoing = pack_rows(groups, tiles, look, observed, row_owner, row_cell)
    arrived = lax.all_to_all(outgoing, ("grp", "tile"), split_axis=0, concat_axis=0, tiled=True)
    sent = edges(place, own, *grp_halos)
    tile_halos = [swap_pairs(block, "tile", first) for first, block in enumerate(sent)]
    mid, side = add_on_nodes(arrived, cap, rows_x, rows_y)
    stress_adjoint, terms = solve(
        place, own, grp_halos, tile_halos, mid, side, cell_element, epochs, groups, tiles
    )
    return stress_adjoint, sum_onto_owner(terms, "tile")


def solution(mesh):
    return jax.shard_map(
        shards,
        mesh=mesh,
        in_specs=(
            P(None, "grp", "tile"),
            P(None, "grp", "tile"),
            P(None, "grp", "tile"),
            P("grp", "tile"),
            P("grp", "tile"),
            P(("grp", "tile"), None),
            P(None, ("grp", "tile"), None),
            P(("grp", "tile"), None),
            P(("grp", "tile")),
        ),
        out_specs=(P(None, "grp", "tile"), P(("grp", "tile"))),
        check_vma=False,
    )
```

```python
import math

import jax
import jax.numpy as jnp
from jax import lax
from jax.experimental import pallas as pl
from jax.experimental.pallas import tpu as pltpu
from jax.sharding import PartitionSpec as P

SWEEPS = 8
PICARD = 2
LANES = 128
FIELDS = 7
REACH = 32
CHUNK = 64
CHUNKS = 8
DELAY = 30
STRIP = 16
MIB = 1024 * 1024
NT = (((1,), (1,)), ((), ()))


def swap_pairs(block, axis, first):
    pairs = [(i, i + 1) for i in range(first, lax.axis_size(axis) - 1, 2)]
    return lax.ppermute(block, axis, pairs + [(b, a) for a, b in pairs])


def thirds(values):
    first = values.astype(jnp.bfloat16)
    rest = values - first.astype(jnp.float32)
    second = rest.astype(jnp.bfloat16)
    third = (rest - second.astype(jnp.float32)).astype(jnp.bfloat16)
    return first, second, third


def one_hot(mask):
    return jnp.where(mask, 1.0, 0.0).astype(jnp.bfloat16)


def rows_kernel(groups, tiles, cap, look_ref, obs_ref, owner_ref, cell_ref, out_ref, pad_ref):
    rows = obs_ref.shape[0]
    devices = groups * tiles
    look_x, look_y, obs = look_ref[0], look_ref[1], obs_ref[...]
    lane = lax.broadcasted_iota(jnp.int32, (rows, LANES), 1)
    sums = jnp.zeros((rows, LANES), jnp.float32)
    for place, (a, b) in enumerate(
        ((look_x, look_x), (look_x, look_y), (look_y, look_y), (look_x, obs), (look_y, obs))
    ):
        sums = jnp.where(lane == place, jnp.sum(a * b, axis=1, keepdims=True), sums)
    sums = sums.T[:8]
    owner = owner_ref[...]
    cell = cell_ref[...]
    named = lax.broadcasted_iota(jnp.int32, (devices, rows), 0) == owner
    before = lax.broadcasted_iota(jnp.int32, (rows, rows), 0) < lax.broadcasted_iota(
        jnp.int32, (rows, rows), 1
    )
    ranks = jnp.dot(one_hot(named), one_hot(before), preferred_element_type=jnp.float32)
    rank = jnp.sum(jnp.where(named, ranks, 0.0), axis=0, keepdims=True)
    slot = owner * cap + rank.astype(jnp.int32)
    hit = one_hot(lax.broadcasted_iota(jnp.int32, (devices * cap, rows), 0) == slot)
    cells = jnp.concatenate(
        [
            lax.shift_right_logical(cell, 7),
            jnp.bitwise_and(cell, 127),
            jnp.zeros((6, rows), jnp.int32),
        ],
        axis=0,
    ).astype(jnp.float32)
    s0, s1, s2 = thirds(sums)
    left = jnp.concatenate(
        [s0.astype(jnp.float32), s1.astype(jnp.float32), s2.astype(jnp.float32), cells], axis=0
    ).astype(jnp.bfloat16)
    placed = lax.dot_general(left, hit, NT, preferred_element_type=jnp.float32)
    table = placed[:8] + placed[8:16] + placed[16:24]
    row = lax.broadcasted_iota(jnp.int32, table.shape, 0)
    table = jnp.where(row == 5, placed[24:25] * 128.0 + placed[25:26], table)
    edge = jnp.zeros((8, LANES), jnp.float32)
    pad_ref[:, :LANES] = edge
    pad_ref[:, LANES : LANES + devices * cap] = table
    pad_ref[:, LANES + devices * cap :] = edge
    lane8 = lax.broadcasted_iota(jnp.int32, (8, LANES), 1)
    row8 = lax.broadcasted_iota(jnp.int32, (8, LANES), 0)
    tail = (lane8 >= 3 * cap) & (lane8 < 4 * cap) & (row8 < 6)
    packed = tail | (row8 >= 6)
    pieces = {}
    for g in range(groups):
        for t in range(tiles):
            start = (g * tiles + t - 1) * cap + LANES
            base, off = start // LANES * LANES, start % LANES
            piece = pad_ref[:, base : base + LANES]
            if off:
                after = pad_ref[:, base + LANES : base + 2 * LANES]
                piece = jnp.where(
                    lane8 < LANES - off,
                    pltpu.roll(piece, LANES - off, 1),
                    pltpu.roll(after, LANES - off, 1),
                )
            low = cap if t == 0 else 0
            high = 2 * cap if t == tiles - 1 else 3 * cap
            piece = jnp.where((lane8 >= low) & (lane8 < high), piece, 0.0)
            turned = jnp.where(row8 < 6, pltpu.roll(piece, 3 * cap, 1), 0.0)
            shared = jnp.where(row8 < 6, pltpu.roll(piece, 2 * cap, 1), 0.0)
            for f in range(6):
                spread = jnp.broadcast_to(piece[f : f + 1], (8, LANES))
                spread = pltpu.roll(spread, (f % 4 - 2) * cap % LANES, 1) if f % 4 != 2 else spread
                group = (lane8 >= f % 4 * cap) & (lane8 < f % 4 * cap + cap) & (row8 == 6 + f // 4)
                turned = jnp.where(group, spread, turned)
            pieces[g, t] = piece, turned, shared
    for g in range(groups):
        for t in range(tiles):
            top = pieces[g - 1, t][0] if g else edge
            low = pieces[g, t][0]
            if g < groups - 1:
                _, turned, shared = pieces[g + 1, t]
                top = jnp.where(packed, turned, top)
                low = jnp.where(tail, shared, low)
            out_ref[g * tiles + t, 0:8, :] = top
            out_ref[g * tiles + t, 8:16, :] = low


def pack_rows(groups, tiles, look, observed, row_owner, row_cell):
    rows = observed.shape[0]
    devices = groups * tiles
    cap = max(2, 2 * rows // devices)
    return pl.pallas_call(
        lambda *refs: rows_kernel(groups, tiles, cap, *refs),
        out_shape=jax.ShapeDtypeStruct((devices, 16, LANES), jnp.float32),
        scratch_shapes=[pltpu.VMEM((8, devices * cap + 2 * LANES), jnp.float32)],
        compiler_params=pltpu.CompilerParams(vmem_limit_bytes=12 * MIB),
        cost_estimate=pl.CostEstimate(flops=4_000_000, bytes_accessed=80_000_000, transcendentals=0),
        name="row_sums",
    )(look, observed, row_owner.reshape(1, rows), row_cell.reshape(1, rows))


def nodes_kernel(cap, rows_x, rows_y, in_ref, mid_ref, side_ref, left_ref, right_ref):
    devices = in_ref.shape[0]
    per = LANES // cap
    slots = devices * cap
    shift = rows_y.bit_length() - 1
    lane8 = lax.broadcasted_iota(jnp.int32, (8, LANES), 1)
    row8 = lax.broadcasted_iota(jnp.int32, (8, LANES), 0)
    for d in range(3):
        wide = rows_x if d == 1 else STRIP
        first_x = {0: rows_x - STRIP, 1: 0, 2: 0}[d]
        out_x = {0: 0, 1: STRIP, 2: STRIP + rows_x}[d]
        lists = []
        for dt in range(3):
            parts = []
            for j in range(devices // per):
                part = jnp.zeros((8, LANES), jnp.float32)
                for q in range(per):
                    here = (lane8 >= q * cap) & (lane8 < q * cap + cap)
                    if d == 2 and dt == 2:
                        for f in range(6):
                            source = in_ref[j * per + q, 6 + f // 4 : 7 + f // 4, :]
                            moved = jnp.broadcast_to(source, (8, LANES))
                            turn = (q - f % 4) * cap % LANES
                            moved = pltpu.roll(moved, turn, 1) if turn else moved
                            part = jnp.where(here & (row8 == f), moved, part)
                        continue
                    at = 8 * dt if d == 2 else 8 * d
                    source = in_ref[j * per + q, at : at + 8, :]
                    turn = (q - (3 if d == 2 else dt)) * cap % LANES
                    moved = pltpu.roll(source, turn, 1) if turn else source
                    part = jnp.where(here & (row8 < 6), moved, part)
                parts.append(part)
            lists.append(jnp.concatenate(parts, axis=1))
        for where, out_ref, width in (((1,), mid_ref, rows_y), ((0, 2), side_ref, LANES)):
            for position, dt in enumerate(where):
                values = lists[dt]
                cell = values[5:6].astype(jnp.int32)
                cell_x = lax.shift_right_logical(cell, shift) - first_x
                cell_y = jnp.bitwise_and(cell, rows_y - 1)
                begin = position * slots
                in_x = lax.broadcasted_iota(jnp.int32, (wide, slots), 0) == cell_x
                pieces = thirds(values)
                for p in range(3):
                    piece = pieces[p].astype(jnp.float32)
                    for f in range(5):
                        at = (p * 5 + f) * wide
                        left_ref[at : at + wide, begin : begin + slots] = jnp.where(
                            in_x, piece[f : f + 1], 0.0
                        ).astype(jnp.bfloat16)
                if dt == 0:
                    cell_y = cell_y - (rows_y - LANES)
                    cell_y = jnp.where(cell_y >= LANES - STRIP, cell_y, -1)
                if dt == 2:
                    cell_y = jnp.where(cell_y < STRIP, cell_y, -1)
                right_ref[:width, begin : begin + slots] = one_hot(
                    lax.broadcasted_iota(jnp.int32, (width, slots), 0) == cell_y
                )
            total = len(where) * slots
            added = lax.dot_general(
                left_ref[: 15 * wide, :total],
                right_ref[:width, :total],
                NT,
                preferred_element_type=jnp.float32,
            )
            added = added[: 5 * wide] + added[5 * wide : 10 * wide] + added[10 * wide :]
            for f in range(5):
                out_ref[f, out_x : out_x + wide, :] = added[f * wide : (f + 1) * wide]


def add_on_nodes(arrived, cap, rows_x, rows_y):
    slots = arrived.shape[0] * cap
    high = rows_x + 2 * STRIP
    return pl.pallas_call(
        lambda *refs: nodes_kernel(cap, rows_x, rows_y, *refs),
        out_shape=(
            jax.ShapeDtypeStruct((5, high, rows_y), jnp.float32),
            jax.ShapeDtypeStruct((5, high, LANES), jnp.float32),
        ),
        scratch_shapes=[
            pltpu.VMEM((15 * rows_x, 2 * slots), jnp.bfloat16),
            pltpu.VMEM((rows_y, 2 * slots), jnp.bfloat16),
        ],
        compiler_params=pltpu.CompilerParams(vmem_limit_bytes=16 * MIB),
        cost_estimate=pl.CostEstimate(flops=4_000_000, bytes_accessed=4_000_000, transcendentals=0),
        name="add_on_nodes",
    )(arrived)


def edges_kernel(*refs):
    heads, tails, (even_ref, odd_ref) = refs[:3], refs[3:6], refs[6:]
    lane = lax.broadcasted_iota(jnp.int32, (8, LANES), 1)
    odd_grp = jnp.broadcast_to(lax.axis_index("grp") % 2 == 1, lane.shape)
    odd_tile = jnp.broadcast_to(lax.axis_index("tile") % 2 == 1, lane.shape)

    def pick(parts, block, f):
        own, even, odd = [part[f, block % 4 * 8 : block % 4 * 8 + 8, :] for part in parts]
        return (jnp.where(odd_grp, even, odd), own, jnp.where(odd_grp, odd, even))[block // 4]

    for f in range(FIELDS):
        for b in range(3):
            begin = jnp.zeros((8, LANES), jnp.float32)
            end = jnp.zeros((8, LANES), jnp.float32)
            for k in range(4):
                block = 3 * k + b
                mine = (lane >= 32 * k) & (lane < 32 * k + 32)
                head, tail = pick(heads, block, f), pick(tails, block, f)
                if k:
                    head = pltpu.roll(head, 32 * k, 1)
                if k != 3:
                    tail = pltpu.roll(tail, 32 * k + 32, 1)
                begin = jnp.where(mine, head, begin)
                end = jnp.where(mine, tail, end)
            even_ref[f, b * 8 : b * 8 + 8, :] = jnp.where(odd_tile, begin, end)
            odd_ref[f, b * 8 : b * 8 + 8, :] = jnp.where(odd_tile, end, begin)


def edges(own, even, odd):
    shape = jax.ShapeDtypeStruct((FIELDS, 24, LANES), jnp.float32)
    part = (FIELDS, own.shape[1], LANES)
    last = own.shape[2] // LANES - 1
    head = pl.BlockSpec(part, lambda i: (0, 0, 0))
    tail = pl.BlockSpec(part, lambda i: (0, 0, last))
    whole = pl.BlockSpec(shape.shape, lambda i: (0, 0, 0))
    return pl.pallas_call(
        edges_kernel,
        grid=(1,),
        in_specs=[head] * 3 + [tail] * 3,
        out_specs=(whole, whole),
        out_shape=(shape, shape),
        compiler_params=pltpu.CompilerParams(vmem_limit_bytes=4 * MIB),
        cost_estimate=pl.CostEstimate(flops=100_000_000_000, bytes_accessed=500_000, transcendentals=0),
        name="edges",
    )(own, even, odd, own, even, odd)


def tile_rows(row, count=1):
    return slice(8 * row, 8 * (row + count))


def to_rows(pieces, left, right, store):
    lane = lax.broadcasted_iota(jnp.int32, (8, LANES), 1)
    by_32 = [left] + [pltpu.roll(p, 32, 1) for p in pieces]
    by_96 = [pltpu.roll(p, 96, 1) for p in pieces] + [right]
    for k in range(4):
        store(2 * k, jnp.where(lane < 32, by_32[k], by_32[k + 1]))
        store(2 * k + 1, jnp.where(lane < 96, by_96[k], by_96[k + 1]))


def from_rows(load):
    lane = lax.broadcasted_iota(jnp.int32, (8, LANES), 1)
    return [
        jnp.where(lane < CHUNK, pltpu.roll(load(2 * k), 96, 1), pltpu.roll(load(2 * k + 1), 32, 1))
        for k in range(4)
    ]


def stencil_rows(load_u, load_v, visc, first_row, last_row, finish):
    ahead = {}
    waiting = []

    def issue(row):
        if row <= last_row + 1:
            ahead[row] = (
                pltpu.roll(load_u(row), LANES - 1, 1),
                pltpu.roll(load_v(row), LANES - 1, 1),
            )

    def lateral(row):
        u, v = load_u(row), load_v(row)
        u_next, v_next = ahead.pop(row)
        return u + u_next, u_next - u, v + v_next, v_next - v

    def stresses(row, here, after):
        half, quarter = visc(row)
        x_u, y_u = after[0] - here[0], after[1] + here[1]
        x_v, y_v = after[2] - here[2], after[3] + here[3]
        both = x_u + y_v
        return half * (x_u + both), half * (y_v + both), quarter * (y_u + x_v)

    def flush():
        row, turned_first, still_first, turned_second, still_second = waiting.pop(0)
        finish(row, load_u(row), load_v(row), turned_first + still_first, turned_second + still_second)

    for row in range(first_row - 1, first_row + 1 + DELAY):
        issue(row)
    before = lateral(first_row - 1)
    here = lateral(first_row)
    below = stresses(first_row - 1, before, here)
    for row in range(first_row, last_row + 1):
        issue(row + 1 + DELAY)
        after = lateral(row + 1)
        above = stresses(row, here, after)
        a, c = below[0] - above[0], below[1] + above[1]
        b, e = below[2] + above[2], below[2] - above[2]
        waiting.append((row, pltpu.roll(a + b, 1, 1), a - b, pltpu.roll(c + e, 1, 1), e - c))
        if len(waiting) > DELAY:
            flush()
        here, below = after, above
    while waiting:
        flush()


def solve_kernel(
    epochs,
    grp_count,
    tile_count,
    own_ref,
    grp_even_ref,
    grp_odd_ref,
    tile_even_ref,
    tile_odd_ref,
    mid_ref,
    side_ref,
    ids_ref,
    out_ref,
    elem_ref,
    field,
    misfit,
    half_q,
    quarter_q,
    keep,
    prec,
    push,
    turn,
    wave_a,
    wave_b,
    seen,
    total,
    fric,
    terms,
):
    rows_x = own_ref.shape[1]
    height = rows_x + 2 * REACH
    grp, tile = lax.axis_index("grp"), lax.axis_index("tile")

    odd_grp = jnp.broadcast_to(grp % 2 == 1, (8, LANES))
    odd_tile = jnp.broadcast_to(tile % 2 == 1, (8, LANES))

    def pick(f, block, j):
        at = (f, slice(block % 4 * 8, block % 4 * 8 + 8), slice(LANES * j, LANES * j + LANES))
        if block // 4 == 1:
            return own_ref[at]
        even, odd = grp_even_ref[at], grp_odd_ref[at]
        return jnp.where(odd_grp, even, odd) if block < 4 else jnp.where(odd_grp, odd, even)

    for f in range(FIELDS):
        for block in range(height // 8):
            k, b = block // 3, block % 3
            even = tile_even_ref[f, b * 8 : b * 8 + 8, :]
            odd = tile_odd_ref[f, b * 8 : b * 8 + 8, :]
            left = jnp.where(odd_tile, even, odd)
            right = jnp.where(odd_tile, odd, even)
            if k:
                left = pltpu.roll(left, LANES - 32 * k, 1)
            if k != 3:
                right = pltpu.roll(right, 96 - 32 * k, 1)

            def store(s, value, f=f, block=block):
                field[f, pl.ds(64 * block + s, 8, stride=8), :] = value

            to_rows([pick(f, block, j) for j in range(4)], left, right, store)
    for f in range(5):
        for block in range((rows_x + 2 * STRIP) // 8):
            at = block * 8
            beyond = side_ref[f, at : at + 8, :]

            def store(s, value, f=f, block=block):
                misfit[f, pl.ds(64 * block + s, 8, stride=8), :] = value

            to_rows(
                [mid_ref[f, at : at + 8, LANES * j : LANES * j + LANES] for j in range(4)],
                pltpu.roll(beyond, 32, 1),
                pltpu.roll(beyond, 96, 1),
                store,
            )

    lane = lax.broadcasted_iota(jnp.int32, (8, LANES), 1)
    chunk = lax.broadcasted_iota(jnp.int32, (8, LANES), 0)
    y = tile * (CHUNK * CHUNKS) + chunk * CHUNK + lane - 32
    in_y = (y >= 0) & (y < tile_count * (CHUNK * CHUNKS))
    in_low = in_y & jnp.broadcast_to(grp > 0, in_y.shape)
    in_high = in_y & jnp.broadcast_to(grp < grp_count - 1, in_y.shape)
    for p, (first_row, last_row) in enumerate(((2, height - 3), (2 + SWEEPS, height - 3 - SWEEPS))):

        def summed(row, p=p):
            e = field[4 + p, tile_rows(row), :]
            return e + pltpu.roll(e, LANES - 1, 1)

        before = summed(first_row - 1)
        row_sum = summed(first_row)
        quad = before + row_sum
        half_q[p, tile_rows(first_row - 1), :] = 0.125 * quad
        quarter_q[p, tile_rows(first_row - 1), :] = 0.0625 * quad
        quad_below = quad + pltpu.roll(quad, 1, 1)
        for row in range(first_row, last_row + 1):
            next_sum = summed(row + 1)
            quad = row_sum + next_sum
            half_q[p, tile_rows(row), :] = 0.125 * quad
            quarter_q[p, tile_rows(row), :] = 0.0625 * quad
            quad_above = quad + pltpu.roll(quad, 1, 1)
            fr = field[6, tile_rows(row), :]
            diagonal = (1.25 * 0.25) * (quad_below + quad_above) + fr
            inside = in_low if row < REACH else in_high if row >= REACH + rows_x else in_y
            pre = jnp.where(inside, 0.45 / diagonal, 0.0)
            prec[p, tile_rows(row), :] = pre
            keep[p, tile_rows(row), :] = 1.0 - pre * fr
            push[p, 0, tile_rows(row), :] = pre * field[2, tile_rows(row), :]
            push[p, 1, tile_rows(row), :] = pre * field[3, tile_rows(row), :]
            if p == 0:
                turn[tile_rows(row), :] = pre * (1.0 / 0.45)
            else:
                turn[tile_rows(row), :] = turn[tile_rows(row), :] * diagonal
            row_sum, quad_below = next_sum, quad_above

    def visc(p):
        return lambda row: (half_q[p, tile_rows(row), :], quarter_q[p, tile_rows(row), :])

    def forward(p, step, source, target, first_row, last_row):
        def finish(row, u, v, first, second):
            at = tile_rows(row)
            pre, rest = prec[p, at, :], keep[p, at, :]
            new_u = rest * u + push[p, 0, at, :] - pre * first
            new_v = rest * v + push[p, 1, at, :] - pre * second
            target(0, row, new_u)
            target(1, row, new_v)
            if REACH <= row < REACH + rows_x:
                here = pl.ds(8 * (row - REACH), 8)
                seen[step, 0, here, :] = new_u - 0.55 * u
                seen[step, 1, here, :] = new_v - 0.55 * v

        stencil_rows(lambda r: source(0, r), lambda r: source(1, r), visc(p), first_row, last_row, finish)

    def reader(ref):
        return lambda c, row: ref[c, tile_rows(row), :]

    def writer(ref):
        def write(c, row, value):
            ref[c, tile_rows(row), :] = value

        return write

    for c in range(2):
        wave_a[c] = field[c]
    for p in range(PICARD):
        rows = (2 + SWEEPS * p, height - 3 - SWEEPS * p)

        def pair(i, _, p=p, rows=rows):
            forward(p, SWEEPS * p + 2 * i, reader(wave_a), writer(wave_b), *rows)
            forward(p, SWEEPS * p + 2 * i + 1, reader(wave_b), writer(wave_a), *rows)
            return 0

        lax.fori_loop(0, SWEEPS // 2, pair, 0)

    first_row, last_row = 17, height - 18
    for row in range(first_row, last_row + 1):
        at, mis = tile_rows(row), tile_rows(row - (REACH - STRIP))
        u, v = wave_a[0, at, :], wave_a[1, at, :]
        cross = misfit[1, mis, :]
        scale = prec[1, at, :] * (1.0 / math.sqrt(epochs))
        wave_a[0, at, :] = scale * (misfit[0, mis, :] * u + cross * v - misfit[3, mis, :])
        wave_a[1, at, :] = scale * (cross * u + misfit[2, mis, :] * v - misfit[4, mis, :])
    total[...] = jnp.zeros_like(total)
    fric[...] = jnp.zeros_like(fric)

    def gather(step, source):
        for row in range(REACH, REACH + rows_x):
            here = tile_rows(row - REACH)
            u, v = source(0, row), source(1, row)
            total[0, here, :] = total[0, here, :] + u
            total[1, here, :] = total[1, here, :] + v
            fric[here, :] = fric[here, :] - (u * seen[step, 0, here, :] + v * seen[step, 1, here, :])

    def backward(p, step, source, target, first_row, last_row, switch=False):
        def finish(row, u, v, first, second):
            at = tile_rows(row)
            pre, rest = prec[p, at, :], keep[p, at, :]
            new_u, new_v = rest * u - pre * first, rest * v - pre * second
            if switch:
                new_u, new_v = new_u * turn[at, :], new_v * turn[at, :]
            target(0, row, new_u)
            target(1, row, new_v)
            if REACH <= row < REACH + rows_x:
                here = tile_rows(row - REACH)
                total[0, here, :] = total[0, here, :] + u
                total[1, here, :] = total[1, here, :] + v
                fric[here, :] = fric[here, :] - (u * seen[step, 0, here, :] + v * seen[step, 1, here, :])

        stencil_rows(lambda r: source(0, r), lambda r: source(1, r), visc(p), first_row, last_row, finish)

    for p in range(PICARD - 1, -1, -1):
        edge = 18 if p == PICARD - 1 else 18 + SWEEPS
        rows = (edge, height - 1 - edge)
        top = SWEEPS * (p + 1) - 1

        def pair(i, _, p=p, rows=rows, top=top):
            backward(p, top - 2 * i, reader(wave_a), writer(wave_b), *rows)
            backward(p, top - 2 * i - 1, reader(wave_b), writer(wave_a), *rows)
            return 0

        lax.fori_loop(0, SWEEPS // 2 - 1, pair, 0)
        backward(p, top - SWEEPS + 2, reader(wave_a), writer(wave_b), *rows)
        if p:
            backward(p, top - SWEEPS + 1, reader(wave_b), writer(wave_a), *rows, switch=True)
        else:
            gather(0, reader(wave_b))

    for block in range(rows_x // 8):
        at = slice(block * 8, block * 8 + 8)
        for c in range(2):
            tiles = from_rows(lambda s: total[c, pl.ds(64 * block + s, 8, stride=8), :])
            for k in range(4):
                out_ref[c, at, LANES * k : LANES * k + LANES] = tiles[k]
        tiles = from_rows(lambda s: fric[pl.ds(64 * block + s, 8, stride=8), :])
        for k in range(4):
            terms[at, LANES * k : LANES * k + LANES] = (
                tiles[k] * (own_ref[6, at, LANES * k : LANES * k + LANES] * (1.0 / 0.45))
            )

    owners, elems = elem_ref.shape
    first_element = grp * (owners * elems)
    width = ids_ref.shape[1]
    owner_at = lax.broadcasted_iota(jnp.int32, (owners, width), 0)
    elem_at = lax.broadcasted_iota(jnp.int32, (elems, width), 0)
    sums = jnp.zeros((3 * owners, elems), jnp.float32)
    for row in range(rows_x):
        local = ids_ref[row : row + 1, :] - first_element
        owner = lax.shift_right_logical(local, 7)
        inside = jnp.bitwise_and(local, elems - 1)
        split = jnp.where(owner_at == owner, terms[row : row + 1, :], 0.0)
        pieces = [piece.astype(jnp.float32) for piece in thirds(split)]
        left = jnp.concatenate(pieces, axis=0).astype(jnp.bfloat16)
        sums = sums + lax.dot_general(
            left, one_hot(elem_at == inside), NT, preferred_element_type=jnp.float32
        )
    elem_ref[...] = sums[:owners] + sums[owners : 2 * owners] + sums[2 * owners :]


def solve(own, grp_halos, tile_halos, mid, side, ids, epochs, grp_count, tile_count):
    rows_x, rows_y = ids.shape
    height = rows_x + 2 * REACH
    elems = LANES
    tall = 8 * height
    spec = pl.BlockSpec(memory_space=pltpu.VMEM)
    f32 = jnp.float32
    return pl.pallas_call(
        lambda *refs: solve_kernel(epochs, grp_count, tile_count, *refs),
        in_specs=[spec] * 8,
        out_specs=(spec, spec),
        out_shape=(
            jax.ShapeDtypeStruct((2, rows_x, rows_y), f32),
            jax.ShapeDtypeStruct((tile_count * rows_x * rows_y // 128 // elems, elems), f32),
        ),
        scratch_shapes=[
            pltpu.VMEM((FIELDS, tall, LANES), f32),
            pltpu.VMEM((5, 8 * (rows_x + 2 * STRIP), LANES), f32),
            pltpu.VMEM((PICARD, tall, LANES), f32),
            pltpu.VMEM((PICARD, tall, LANES), f32),
            pltpu.VMEM((PICARD, tall, LANES), f32),
            pltpu.VMEM((PICARD, tall, LANES), f32),
            pltpu.VMEM((PICARD, 2, tall, LANES), f32),
            pltpu.VMEM((tall, LANES), f32),
            pltpu.VMEM((2, tall, LANES), f32),
            pltpu.VMEM((2, tall, LANES), f32),
            pltpu.VMEM((PICARD * SWEEPS, 2, 8 * rows_x, LANES), f32),
            pltpu.VMEM((2, 8 * rows_x, LANES), f32),
            pltpu.VMEM((8 * rows_x, LANES), f32),
            pltpu.VMEM((rows_x, rows_y), f32),
        ],
        compiler_params=pltpu.CompilerParams(vmem_limit_bytes=28 * MIB),
        cost_estimate=pl.CostEstimate(
            flops=80_000_000, bytes_accessed=4_000_000, transcendentals=0
        ),
        name="solve",
    )(own, *grp_halos, *tile_halos, mid, side, ids)


def sum_onto_owner(terms, axis):
    count = lax.axis_size(axis)
    me = lax.axis_index(axis)
    span = 1
    terms = terms.reshape((count, 1, -1))
    while span < count:
        halves = terms.reshape((terms.shape[0] // 2, 2, -1))
        bit = me // span % 2
        mine = lax.dynamic_index_in_dim(halves, bit, 1, keepdims=False)
        other = lax.dynamic_index_in_dim(halves, 1 - bit, 1, keepdims=False)
        terms = mine + lax.ppermute(other, axis, [(i, i ^ span) for i in range(count)])
        span *= 2
    return terms.reshape(-1)


def shards(
    start_velocity,
    driving_stress,
    viscosity,
    friction,
    cell_element,
    observed,
    look,
    row_owner,
    row_cell,
):
    rows_x, rows_y = friction.shape
    row_dev, epochs = observed.shape
    groups, tiles = lax.axis_size("grp"), lax.axis_size("tile")
    devices = groups * tiles
    cap = max(2, 2 * row_dev // devices)
    own = jnp.concatenate([start_velocity, driving_stress, viscosity, friction[None]], axis=0)
    grp_halos = [swap_pairs(own, "grp", first) for first in (0, 1)]
    outgoing = pack_rows(groups, tiles, look, observed, row_owner, row_cell)
    arrived = lax.all_to_all(outgoing, ("grp", "tile"), split_axis=0, concat_axis=0, tiled=True)
    sent = edges(own, *grp_halos)
    tile_halos = [swap_pairs(block, "tile", first) for first, block in enumerate(sent)]
    mid, side = add_on_nodes(arrived, cap, rows_x, rows_y)
    stress_adjoint, terms = solve(
        own, grp_halos, tile_halos, mid, side, cell_element, epochs, groups, tiles
    )
    return stress_adjoint, sum_onto_owner(terms, "tile")


def solution(mesh):
    return jax.shard_map(
        shards,
        mesh=mesh,
        in_specs=(
            P(None, "grp", "tile"),
            P(None, "grp", "tile"),
            P(None, "grp", "tile"),
            P("grp", "tile"),
            P("grp", "tile"),
            P(("grp", "tile"), None),
            P(None, ("grp", "tile"), None),
            P(("grp", "tile"), None),
            P(("grp", "tile")),
        ),
        out_specs=(P(None, "grp", "tile"), P(("grp", "tile"))),
        check_vma=False,
    )
```
